512 devices in a mesh: traj: 128 (over y, z, core), var: 4 (over x).
Axes of the slice: x: 4, y: 4, z: 16, core: 2. Of those that a mesh axis runs over, the one named last changes fastest.
Arguments:
- series: bfloat16 [393216, 1024], P('traj', 'var'), may hold values from -6 to 6
- lengths: int32 [512], P('traj'), may hold values from 64 to 2048, as said below
- tile_owner: int32 [3072], P('traj'), may hold values from 0 to 4, as said below
- factor_h: float32 [64, 64], replicated, as said below
- factor_v: float32 [64, 1024], P(None, 'var'), may hold values from -6 to 6
- weights_s: float32 [64, 512], P(None, 'traj'), may hold values from 0.5 to 2
Outputs:
- new_h: float32 [64, 64], replicated
- new_v: float32 [64, 1024], P(None, 'var')
- new_s: float32 [64, 512], P(None, 'traj')
The draws below stay inside these ranges and needn't reach their ends.
Inputs may be any that keep to these rules, and one draw needn't show every extreme that they name: `lengths`: each length is a multiple of 64 and needs at most 1 + (length - 1) // 128 tile slots; the longest length in a draw is exactly the maximum. `tile_owner`: on each index of traj, trajectory j takes the next 1 + (length - 1) // 128 slots after those of trajectories 0 to j - 1, starting at slot 0; the remaining slots hold 4. Some index of traj uses all 24 slots. `factor_h`: A square matrix of full rank.
All inputs are finite; a program needn't handle non-finite values.
Results may differ from the reference program's by a relative error of at most 0.0031.
Values may be sent and summed in bfloat16 or wider, within the bound.
No kernel may reach another device: no remote copies, remote signals or barrier semaphores. Data moves between devices by JAX's collectives and lax.ppermute only.
A program may use at most 64 MiB of HBM per device.

```python
import math
import jax
import jax.numpy as jnp
from jax import lax

J = 1024
R = 64
TILE = 128
LMAX = 2048
ITERS = 8
K_DEV = 4
TILES = 24
K = 512
ROWS = 393216
N_TRAJ = 128


def tile_plan(key):
    devices = K // K_DEV
    most_tiles = LMAX // TILE
    tile_cap = min(most_tiles, TILES - 3)
    key_first, key_second, key_trim, key_busiest, key_fill = jax.random.split(key, 5)
    first_draw = jax.random.randint(key_first, (devices, K_DEV), 0, 16)
    second_draw = jax.random.randint(key_second, (devices, K_DEV), 0, 16)
    wanted = 1 + first_draw * second_draw * most_tiles // 192
    used_tiles = jnp.zeros((devices,), jnp.int32)
    columns = []
    for column_index in range(K_DEV):
        free_room = TILES - used_tiles - (K_DEV - 1 - column_index)
        granted = jnp.minimum(jnp.minimum(wanted[:, column_index], tile_cap), free_room)
        columns.append(granted)
        used_tiles = used_tiles + granted
    busiest = jax.random.randint(key_busiest, (), 0, devices)
    full_counts = [jnp.full((), tile_cap, jnp.int32)]
    remaining = jnp.full((), TILES - tile_cap, jnp.int32)
    fill_keys = jax.random.split(key_fill, K_DEV)
    for column_index in range(1, K_DEV):
        later = K_DEV - 1 - column_index
        low_bound = jnp.maximum(1, remaining - tile_cap * later)
        high_bound = jnp.minimum(tile_cap, remaining - later)
        granted = jax.random.randint(fill_keys[column_index], (), low_bound, high_bound + 1)
        full_counts.append(granted)
        remaining = remaining - granted
    counts = jnp.stack(columns, axis=1)
    is_busiest = (jnp.arange(devices) == busiest)[:, None]
    counts = jnp.where(is_busiest, jnp.stack(full_counts)[None, :], counts)
    trimmed = jax.random.randint(key_trim, (devices, K_DEV), 0, 2)
    trimmed = jnp.where(is_busiest & (jnp.arange(K_DEV) == 0)[None, :], 0, trimmed)
    return (counts, trimmed)


def draw_lengths(key, part):
    counts, trimmed = tile_plan(key)
    return ((2 * counts - trimmed) * (TILE // 2)).reshape(K).astype(jnp.int32)


def draw_tile_owner(key, part):
    counts, trimmed = tile_plan(key)
    ends = jnp.cumsum(counts, axis=1)
    positions = jnp.arange(TILES, dtype=jnp.int32)
    owner = jnp.sum((positions[None, :, None] >= ends[:, None, :]).astype(jnp.int32), axis=2)
    return owner.reshape(K // K_DEV * TILES).astype(jnp.int32)


def draw_factor_h(key, part):
    key = jax.random.fold_in(key, 7)
    key_diag, key_off = jax.random.split(key)
    diagonal = jax.random.uniform(key_diag, (R,), jnp.float32, 1.5, 2.5)
    off_diag = jnp.clip(jax.random.normal(key_off, (R, R), jnp.float32), -4.0, 4.0) * 0.06
    return jnp.eye(R, dtype=jnp.float32) * diagonal[None, :] + off_diag


def steps_of(stream_key, dims, pieces, low, top_value):
    factor_of = 1.0
    for axis_at, blocks in pieces:
        heights = jax.random.uniform(jax.random.fold_in(jax.random.fold_in(stream_key, 6), axis_at), (blocks,), jnp.float32, low / len(pieces), top_value / len(pieces))
        factor_of = factor_of * jnp.repeat(jnp.exp(heights), dims[axis_at] // blocks).reshape((-1,) + (1,) * (len(dims) - 1 - axis_at))
    return factor_of


def scatter_about(own_key, shape, width, bound, cuts=(), kind=jnp.bfloat16):
    array = jax.random.normal(own_key, shape, jnp.float32) * width
    if len(cuts) > 0:
        array = steps_of(own_key, shape, cuts, -0.22, 0.18) * array
    return jnp.clip(array, min=-bound, max=bound).astype(kind)


def setup_inputs(seed: int = 0) -> dict:
    key_list = jax.random.split(jax.random.key(seed), 7)
    series = scatter_about(key_list[0], (ROWS, J), 1.0, 6.0, ((0, 128), (1, 4)))
    lengths = draw_lengths(jax.random.fold_in(key_list[6], 71), 0)
    tile_owner = draw_tile_owner(jax.random.fold_in(key_list[6], 71), 0)
    factor_h = draw_factor_h(jax.random.fold_in(key_list[6], 71), 0)
    factor_v = scatter_about(key_list[4], (R, J), 1.0, 6.0, ((1, 4),), jnp.float32)
    weights_s = jnp.clip(jnp.exp(math.log(2.0) - 1.3862944 * jax.random.uniform(key_list[5], (R, K), jnp.float32) ** steps_of(key_list[5], (R, K), ((1, 128),), -0.2, 0.2)), 0.5, 2.0)
    return dict(series=series, lengths=lengths, tile_owner=tile_owner, factor_h=factor_h, factor_v=factor_v, weights_s=weights_s)


highest = lax.Precision.HIGHEST

def layout(owner, lengths, tile_len):
    slot_ids = jnp.arange(lengths.shape[0], dtype=jnp.int32)
    member = owner[:, None] == slot_ids[None, :]
    starts = lax.optimization_barrier(jnp.sum((owner[:, None] < slot_ids[None, :]).astype(jnp.int32), axis=0))
    first_slot = lax.optimization_barrier(jnp.sum(jnp.where(member, starts[None, :], 0), axis=1))
    limit = lax.optimization_barrier(jnp.sum(jnp.where(member, lengths[None, :], 0), axis=1))
    tile_ids = jnp.arange(owner.shape[0], dtype=jnp.int32)
    place = (tile_ids - first_slot)[:, None] * tile_len + jnp.arange(tile_len, dtype=jnp.int32)[None, :]
    live = (place < limit[:, None]).astype(jnp.float32)
    return (member.astype(jnp.float32), live)

def keep_same(value):
    return value

def polar_factor(partial_value, mixers, member, live, gram_total, norm_total):
    mixed = jnp.einsum('tk,kab->tab', member, mixers, precision=highest)
    target = jnp.einsum('tab,tbs->tas', mixed, partial_value * live[:, None, :], precision=highest)
    energy = norm_total(jnp.einsum('tk,t->k', member, lax.optimization_barrier(jnp.sum(target * target, axis=(1, 2))), precision=highest))
    scales = jnp.dot(member, lax.rsqrt(energy + 1e-06), precision=highest)
    current = target * scales[:, None, None]
    for iteration in range(ITERS):
        tile_grams = jnp.einsum('tas,tbs->tab', current, current, precision=highest)
        grams = gram_total(jnp.einsum('tk,tab->kab', member, tile_grams, precision=highest))
        spread = jnp.einsum('tk,kab->tab', member, grams, precision=highest)
        current = 1.5 * current - 0.5 * jnp.einsum('tab,tbs->tas', spread, current, precision=highest)
    return current.astype(jnp.bfloat16)

def chol_solve(gram, right):
    lower = jnp.linalg.cholesky(gram)
    middle = lax.linalg.triangular_solve(lower, right, left_side=True, lower=True)
    return lax.linalg.triangular_solve(lower, middle, left_side=True, lower=True, transpose_a=True)

def block_slices(series_block, owner_block, length_block, weight_block, factor_h, factor_bf):
    tile_total = owner_block.shape[0]
    blocks = series_block.reshape(tile_total, -1, series_block.shape[1])
    member, live = layout(owner_block, length_block, blocks.shape[1])
    partial_value = jnp.einsum('rj,tsj->trs', factor_bf.astype(jnp.float32), blocks.astype(jnp.float32), precision=highest)
    mixers = factor_h[None, :, :] * weight_block.T[:, None, :]
    polar = polar_factor(partial_value, mixers, member, live, keep_same, keep_same)
    per_tile = jnp.einsum('trs,tsj->trj', polar.astype(jnp.float32), blocks.astype(jnp.float32), precision=highest)
    return jnp.einsum('tk,trj->krj', member, per_tile, precision=highest)

def reference(series, lengths, tile_owner, factor_h, factor_v, weights_s):
    factor_bf = factor_v.astype(jnp.bfloat16)
    series_all = series.reshape(N_TRAJ, TILES * TILE, J)
    owners = tile_owner.reshape(N_TRAJ, TILES)
    length_rows = lengths.reshape(N_TRAJ, K_DEV)
    weight_blocks = jnp.transpose(weights_s.reshape(R, N_TRAJ, K_DEV), (1, 0, 2))

    def one_block(items):
        return block_slices(items[0], items[1], items[2], items[3], factor_h, factor_bf)
    projected = lax.map(one_block, (series_all, owners, length_rows, weight_blocks)).reshape(K, R, J)
    head_part = jnp.einsum('kaj,rj->kar', projected, factor_v, precision=highest)
    head_terms = jnp.einsum('kar,rk->ar', head_part, weights_s, precision=highest)
    factor_gram = jnp.dot(factor_v, factor_v.T, precision=highest)
    weight_gram = jnp.dot(weights_s, weights_s.T, precision=highest)
    new_h = chol_solve(factor_gram * weight_gram, head_terms.T).T
    scaled = new_h[None, :, :] * weights_s.T[:, None, :]
    column_terms = jnp.einsum('kar,kaj->rj', scaled, projected, precision=highest)
    head_gram = jnp.dot(new_h.T, new_h, precision=highest)
    new_v = chol_solve(head_gram * weight_gram, column_terms)
    along = jnp.einsum('kaj,rj->kar', projected, new_v, precision=highest)
    weight_terms = jnp.einsum('kar,ar->rk', along, new_h, precision=highest)
    new_s = chol_solve(head_gram * jnp.dot(new_v, new_v.T, precision=highest), weight_terms)
    return (new_h, new_v, new_s)
```

```python
import functools

import jax
import jax.numpy as jnp
from jax import lax
from jax.experimental import pallas as pl
from jax.experimental.pallas import tpu as pltpu
from jax.sharding import Mesh, PartitionSpec as P

ITERS = 8
R = 64
TILE = 128
KD = 4
LANES = (((1,), (1,)), ((), ()))

highest = lax.Precision.HIGHEST


def mm(left, right):
    return jnp.dot(left, right, precision=highest, preferred_element_type=jnp.float32)


def mm_t(left, right):
    return lax.dot_general(left, right, LANES, precision=highest, preferred_element_type=jnp.float32)


def eye_mask():
    rows = lax.broadcasted_iota(jnp.int32, (R, R), 0)
    cols = lax.broadcasted_iota(jnp.int32, (R, R), 1)
    return rows == cols


def eliminate(both):
    rows = lax.broadcasted_iota(jnp.int32, both.shape, 0)
    for k in range(R):
        row = both[k : k + 1, :] / both[k : k + 1, k : k + 1]
        both = jnp.where(rows == k, row, both - both[:, k : k + 1] * row)
    return both


def partial_kernel(v_ref, s_ref, out_ref):
    value = lax.dot_general(
        v_ref[...].astype(jnp.bfloat16), s_ref[...], LANES, preferred_element_type=jnp.float32
    ).astype(jnp.bfloat16)
    for peer in range(out_ref.shape[0]):
        out_ref[peer] = value


def polar_kernel(
    owner_ref, length_ref, part_ref, s_ref, h_ref, v_ref, w_ref, proj_ref, pack_ref, p_ref, g_ref, q_ref, *, peers, spread
):
    slots = s_ref.shape[0] // TILE
    eye = eye_mask()
    lane = lax.broadcasted_iota(jnp.int32, (R, TILE), 1)
    starts = [jnp.int32(0)]
    for k in range(1, KD):
        total = jnp.int32(0)
        for t in range(slots):
            total = total + jnp.where(owner_ref[t] < k, 1, 0)
        starts.append(total)
    g_ref[...] = jnp.zeros_like(g_ref)
    q_ref[...] = jnp.zeros_like(q_ref)
    for t in range(slots):
        own = owner_ref[t]
        left = jnp.int32(0)
        for k in range(KD):
            left = jnp.where(own == k, length_ref[k] - (t - starts[k]) * TILE, left)
        cols = slice(t * TILE, (t + 1) * TILE)
        value = part_ref[0, :, cols].astype(jnp.float32)
        for peer in range(1, peers):
            value = value + part_ref[peer, :, cols].astype(jnp.float32)
        value = jnp.where(lane < left, value, 0.0)
        p_ref[:, cols] = value
        g_ref[own] += mm_t(value, value)
    hmat = h_ref[...]
    wmat = w_ref[...]
    grams, turns = [], []
    for k in range(KD):
        mix = hmat * jnp.sum(jnp.where(eye, wmat[:, k : k + 1], 0.0), axis=0, keepdims=True)
        gram = mm_t(mm(mix, g_ref[k]), mix)
        energy = jnp.sum(jnp.where(eye, gram, 0.0), keepdims=True)
        scale = lax.rsqrt(energy + 1e-06)
        grams.append(gram * (scale * scale))
        turns.append(mix * scale)
    for iteration in range(ITERS):
        steps = [jnp.where(eye, 1.5, 0.0) - 0.5 * gram for gram in grams]
        turns = [mm(step, turn) for step, turn in zip(steps, turns)]
        if iteration < ITERS - 1:
            halves = [mm(step, gram) for step, gram in zip(steps, grams)]
            grams = [mm(half, step) for half, step in zip(halves, steps)]
    for k in range(KD):
        g_ref[k] = turns[k]
    for t in range(slots):
        own = owner_ref[t]
        cols = slice(t * TILE, (t + 1) * TILE)
        polar = mm(g_ref[own], p_ref[:, cols]).astype(jnp.bfloat16)
        q_ref[own] += jnp.dot(polar, s_ref[cols, :], preferred_element_type=jnp.float32)
    vmat = v_ref[...]
    width = vmat.shape[1]
    head = jnp.zeros((R, R), jnp.float32)
    for k in range(KD):
        block = q_ref[k]
        proj_ref[:, k * width : (k + 1) * width] = block
        head = head + mm_t(block, vmat * wmat[:, k : k + 1])
    pack_ref[0:R, :] = jnp.concatenate([head, mm_t(wmat, wmat) * (1.0 / peers)], axis=1)
    pack_ref[R : 2 * R, :] = jnp.concatenate(
        [mm_t(vmat, vmat) * (1.0 / spread), jnp.zeros((R, R), jnp.float32)], axis=1
    )


def head_kernel(pack_ref, proj_ref, w_ref, newh_ref, hp_ref, col_ref, side_ref):
    head, wgram = pack_ref[0:R, 0:R], pack_ref[0:R, R : 2 * R]
    fgram = pack_ref[R : 2 * R, 0:R]
    eye = eye_mask()
    newh_t = eliminate(jnp.concatenate([fgram * wgram, head.T], axis=1))[:, R:]
    newh_ref[...] = newh_t.T
    wmat = w_ref[...]
    hp = mm(newh_t, proj_ref[...])
    hp_ref[...] = hp
    width = hp.shape[1] // KD
    col = hp[:, 0:width] * wmat[:, 0:1]
    for k in range(1, KD):
        col = col + hp[:, k * width : (k + 1) * width] * wmat[:, k : k + 1]
    for half in range(width // TILE):
        col_ref[half * R : (half + 1) * R, :] = col[:, half * TILE : (half + 1) * TILE]
    hgram = mm_t(newh_t, newh_t)
    inverse = eliminate(jnp.concatenate([hgram * wgram, jnp.where(eye, 1.0, 0.0)], axis=1))[:, R:]
    side_ref[...] = jnp.concatenate([hgram, inverse], axis=1)


def column_kernel(col_ref, hp_ref, side_ref, newv_ref, out_ref):
    halves = col_ref.shape[0] // R
    col = jnp.concatenate([col_ref[half * R : (half + 1) * R, :] for half in range(halves)], axis=1)
    newv = mm(side_ref[:, R : 2 * R], col)
    newv_ref[...] = newv
    width = newv.shape[1]
    lane = lax.broadcasted_iota(jnp.int32, (R, R), 1)
    terms = jnp.zeros((R, R), jnp.float32)
    for k in range(KD):
        sums = jnp.sum(hp_ref[:, k * width : (k + 1) * width] * newv, axis=1, keepdims=True)
        terms = jnp.where(lane == k, sums, terms)
    value = jnp.concatenate([mm_t(newv, newv), terms], axis=1)
    for peer in range(out_ref.shape[0]):
        out_ref[peer] = value


def weight_kernel(in_ref, side_ref, out_ref):
    value = in_ref[0]
    for peer in range(1, in_ref.shape[0]):
        value = value + in_ref[peer]
    solved = eliminate(jnp.concatenate([side_ref[:, 0:R] * value[:, 0:R], value[:, R : 2 * R]], axis=1))
    out_ref[...] = solved[:, R : R + KD]


def vmem(count):
    return [pl.BlockSpec(memory_space=pltpu.VMEM)] * count


def params():
    return pltpu.CompilerParams(vmem_limit_bytes=48 * 1024 * 1024)


def f32(*shape):
    return jax.ShapeDtypeStruct(shape, jnp.float32)


def exchange(value, axes):
    return lax.all_to_all(value, axes, 0, 0, tiled=True)


def share(value, axes, peers):
    return exchange(jnp.broadcast_to(value[None], (peers,) + value.shape), axes)


def body(sizes, series, lengths, tile_owner, factor_h, factor_v, weights_s):
    ny, nz, nc, nx = sizes
    rows, width = series.shape
    slots = tile_owner.shape[0]
    chunk = rows // 6
    parts = pl.pallas_call(
        partial_kernel,
        grid=(rows // chunk,),
        in_specs=[
            pl.BlockSpec((R, width), lambda i: (0, 0)),
            pl.BlockSpec((chunk, width), lambda i: (i, 0)),
        ],
        out_specs=pl.BlockSpec((nx, R, chunk), lambda i: (0, 0, i)),
        out_shape=jax.ShapeDtypeStruct((nx, R, rows), jnp.bfloat16),
        compiler_params=params(),
    )(factor_v, series)
    parts = exchange(parts, "x")
    proj, pack = pl.pallas_call(
        functools.partial(polar_kernel, peers=nx, spread=ny * nz * nc),
        in_specs=[pl.BlockSpec(memory_space=pltpu.SMEM)] * 2 + vmem(5),
        out_specs=vmem(2),
        out_shape=[f32(R, KD * width), f32(2 * R, 2 * R)],
        scratch_shapes=[
            pltpu.VMEM((R, rows), jnp.float32),
            pltpu.VMEM((KD + 1, R, R), jnp.float32),
            pltpu.VMEM((KD + 1, R, width), jnp.float32),
        ],
        compiler_params=params(),
    )(tile_owner, lengths, parts, series, factor_h, factor_v, weights_s)
    near = ny * nc * nx
    pieces = exchange(pack.reshape(near, 2 * R // near, 2 * R), ("y", "c", "x"))
    pieces = share(jnp.sum(pieces, axis=0), "z", nz)
    pieces = share(jnp.sum(pieces, axis=0), ("y", "c", "x"), near)
    new_h, hp, col, side = pl.pallas_call(
        head_kernel,
        in_specs=vmem(3),
        out_specs=vmem(4),
        out_shape=[f32(R, R), f32(R, KD * width), f32(R * width // TILE, TILE), f32(R, 2 * R)],
        compiler_params=params(),
    )(pieces.reshape(2 * R, 2 * R), proj, weights_s)
    near = ny * nc
    pieces = exchange(col.reshape(near, col.shape[0] // near, TILE), ("y", "c"))
    pieces = share(jnp.sum(pieces, axis=0), "z", nz)
    pieces = share(jnp.sum(pieces, axis=0), ("y", "c"), near)
    new_v, sums = pl.pallas_call(
        column_kernel,
        in_specs=vmem(3),
        out_specs=vmem(2),
        out_shape=[f32(R, width), f32(nx, R, 2 * R)],
        compiler_params=params(),
    )(pieces.reshape(col.shape), hp, side)
    new_s = pl.pallas_call(
        weight_kernel,
        in_specs=vmem(2),
        out_specs=pl.BlockSpec(memory_space=pltpu.VMEM),
        out_shape=f32(R, KD),
        compiler_params=params(),
    )(exchange(sums, "x"), side)
    return (new_h, new_v, new_s)


def solution(mesh):
    traj, nx = mesh.devices.shape
    ny, nc = (4, 2) if traj % 128 == 0 else (2, 2)
    sizes = (ny, traj // (ny * nc), nc, nx)
    fine = Mesh(mesh.devices.reshape(sizes), ("y", "z", "c", "x"))
    traj_axes = ("y", "z", "c")
    return jax.shard_map(
        functools.partial(body, sizes),
        mesh=fine,
        in_specs=(P(traj_axes, "x"), P(traj_axes), P(traj_axes), P(), P(None, "x"), P(None, traj_axes)),
        out_specs=(P(), P(None, "x"), P(None, traj_axes)),
        check_vma=False,
    )
```

```python
import functools

import jax
import jax.numpy as jnp
from jax import lax
from jax.experimental import pallas as pl
from jax.experimental.pallas import tpu as pltpu
from jax.sharding import Mesh, PartitionSpec as P

ITERS = 8
R = 64
TILE = 128
KD = 4
LANES = (((1,), (1,)), ((), ()))

highest = lax.Precision.HIGHEST


def mm(left, right):
    return jnp.dot(left, right, precision=highest, preferred_element_type=jnp.float32)


def mm_t(left, right):
    return lax.dot_general(left, right, LANES, precision=highest, preferred_element_type=jnp.float32)


def eye_mask():
    rows = lax.broadcasted_iota(jnp.int32, (R, R), 0)
    cols = lax.broadcasted_iota(jnp.int32, (R, R), 1)
    return rows == cols


def eliminate(both):
    rows = lax.broadcasted_iota(jnp.int32, both.shape, 0)
    for k in range(0, R, 4):
        col = [jnp.broadcast_to(both[:, k + i : k + i + 1], both.shape) for i in range(4)]
        row = [both[k + i : k + i + 1, :] for i in range(4)]
        piv = [[col[j][k + i : k + i + 1, :] for j in range(4)] for i in range(4)]
        inv = 1.0 / (piv[0][0] * piv[1][1] - piv[0][1] * piv[0][1])
        a00, a01, a11 = piv[1][1] * inv, -piv[0][1] * inv, piv[0][0] * inv
        e02, e12 = a00 * piv[0][2] + a01 * piv[1][2], a01 * piv[0][2] + a11 * piv[1][2]
        e03, e13 = a00 * piv[0][3] + a01 * piv[1][3], a01 * piv[0][3] + a11 * piv[1][3]
        s22 = piv[2][2] - (piv[0][2] * e02 + piv[1][2] * e12)
        s23 = piv[2][3] - (piv[0][2] * e03 + piv[1][2] * e13)
        s33 = piv[3][3] - (piv[0][3] * e03 + piv[1][3] * e13)
        inv = 1.0 / (s22 * s33 - s23 * s23)
        t2 = row[2] - e02 * row[0] - e12 * row[1]
        t3 = row[3] - e03 * row[0] - e13 * row[1]
        n2, n3 = (s33 * t2 - s23 * t3) * inv, (s22 * t3 - s23 * t2) * inv
        n0 = (a00 * row[0] + a01 * row[1]) - e02 * n2 - e03 * n3
        n1 = (a01 * row[0] + a11 * row[1]) - e12 * n2 - e13 * n3
        rest = (both - col[0] * n0 - col[1] * n1) - (col[2] * n2 + col[3] * n3)
        for i, new in enumerate((n0, n1, n2, n3)):
            rest = jnp.where(rows == k + i, new, rest)
        both = rest
    return both


def partial_kernel(v_ref, s_ref, out_ref):
    out_ref[0] = lax.dot_general(
        v_ref[...].astype(jnp.bfloat16), s_ref[...], LANES, preferred_element_type=jnp.float32
    ).astype(jnp.bfloat16)


def three(value):
    high = value.astype(jnp.bfloat16)
    rest = value - high.astype(jnp.float32)
    middle = rest.astype(jnp.bfloat16)
    return high, middle, (rest - middle.astype(jnp.float32)).astype(jnp.bfloat16)


def polar_kernel(
    owner_ref, length_ref, part_ref, s_ref, h_ref, v_ref, w_ref, proj_ref, pack_ref, p_ref, g_ref, t_ref, q_ref, *, peers, spread
):
    slots = s_ref.shape[0] // TILE
    eye = eye_mask()
    lane = lax.broadcasted_iota(jnp.int32, (R, TILE), 1)
    starts = [jnp.int32(0)]
    for k in range(1, KD):
        total = jnp.int32(0)
        for t in range(slots):
            total = total + jnp.where(owner_ref[t] < k, 1, 0)
        starts.append(total)
    g_ref[...] = jnp.zeros_like(g_ref)
    q_ref[...] = jnp.zeros_like(q_ref)
    for t in range(slots):
        own = owner_ref[t]
        left = jnp.int32(0)
        for k in range(KD):
            left = jnp.where(own == k, length_ref[k] - (t - starts[k]) * TILE, left)
        cols = slice(t * TILE, (t + 1) * TILE)
        quarter, first = divmod(t * TILE, part_ref.shape[2])
        value = part_ref[quarter, :, first : first + TILE]
        value = jnp.where(lane < left, value.astype(jnp.float32), 0.0).astype(jnp.bfloat16)
        p_ref[:, cols] = value
        g_ref[own] += lax.dot_general(value, value, LANES, preferred_element_type=jnp.float32)
    hmat = h_ref[...]
    wmat = w_ref[...].T
    grams, turns = [], []
    for k in range(KD):
        mix = hmat * jnp.sum(jnp.where(eye, wmat[:, k : k + 1], 0.0), axis=0, keepdims=True)
        gram = mm_t(mm(mix, g_ref[k]), mix)
        energy = jnp.sum(jnp.where(eye, gram, 0.0), keepdims=True)
        scale = lax.rsqrt(energy + 1e-06)
        grams.append(gram * (scale * scale))
        turns.append(mix * scale)
    for iteration in range(ITERS):
        steps = [jnp.where(eye, 1.5, 0.0) - 0.5 * gram for gram in grams]
        turns = [mm(step, turn) for step, turn in zip(steps, turns)]
        if iteration < ITERS - 1:
            halves = [mm(step, gram) for step, gram in zip(steps, grams)]
            grams = [mm(half, step) for half, step in zip(halves, steps)]
    t_ref[KD] = jnp.zeros_like(t_ref[KD])
    for k in range(KD):
        for i, term in enumerate(three(turns[k])):
            t_ref[k, i] = term
    for t in range(slots):
        own = owner_ref[t]
        cols = slice(t * TILE, (t + 1) * TILE)
        value = p_ref[:, cols]
        terms = [jnp.dot(t_ref[own, i], value, preferred_element_type=jnp.float32) for i in range(3)]
        polar = (terms[0] + (terms[1] + terms[2])).astype(jnp.bfloat16)
        q_ref[own] += jnp.dot(polar, s_ref[cols, :], preferred_element_type=jnp.float32)
    vmat = v_ref[...]
    width = vmat.shape[1]
    head = jnp.zeros((R, R), jnp.float32)
    for k in range(KD):
        block = q_ref[k]
        proj_ref[:, k * width : (k + 1) * width] = block
        head = head + mm_t(block, vmat * wmat[:, k : k + 1])
    pack_ref[0:R, :] = jnp.concatenate([head, mm_t(wmat, wmat) * (1.0 / peers)], axis=1)
    pack_ref[R : 2 * R, :] = jnp.concatenate(
        [mm_t(vmat, vmat) * (1.0 / spread), jnp.zeros((R, R), jnp.float32)], axis=1
    )


def head_kernel(pack_ref, proj_ref, w_ref, newh_ref, hp_ref, col_ref, side_ref):
    head, wgram = pack_ref[0:R, 0:R], pack_ref[0:R, R : 2 * R]
    fgram = pack_ref[R : 2 * R, 0:R]
    eye = eye_mask()
    newh_t = eliminate(jnp.concatenate([fgram * wgram, head.T], axis=1))[:, R:]
    newh_ref[...] = newh_t.T
    wmat = w_ref[...].T
    hp = mm(newh_t, proj_ref[...])
    hp_ref[...] = hp
    width = hp.shape[1] // KD
    col = hp[:, 0:width] * wmat[:, 0:1]
    for k in range(1, KD):
        col = col + hp[:, k * width : (k + 1) * width] * wmat[:, k : k + 1]
    for half in range(width // TILE):
        col_ref[half * R : (half + 1) * R, :] = col[:, half * TILE : (half + 1) * TILE]
    hgram = mm_t(newh_t, newh_t)
    inverse = eliminate(jnp.concatenate([hgram * wgram, jnp.where(eye, 1.0, 0.0)], axis=1))[:, R:]
    side_ref[...] = jnp.concatenate([hgram, inverse], axis=1)


def column_kernel(col_ref, hp_ref, side_ref, newv_ref, out_ref):
    halves = col_ref.shape[0] // R
    col = jnp.concatenate([col_ref[half * R : (half + 1) * R, :] for half in range(halves)], axis=1)
    newv = mm(side_ref[:, R : 2 * R], col)
    newv_ref[...] = newv
    width = newv.shape[1]
    lane = lax.broadcasted_iota(jnp.int32, (R, R), 1)
    terms = jnp.zeros((R, R), jnp.float32)
    for k in range(KD):
        sums = jnp.sum(hp_ref[:, k * width : (k + 1) * width] * newv, axis=1, keepdims=True)
        terms = jnp.where(lane == k, sums, terms)
    value = jnp.concatenate([mm_t(newv, newv), terms], axis=1)
    for peer in range(out_ref.shape[0]):
        out_ref[peer] = value


def weight_kernel(in_ref, side_ref, out_ref):
    value = in_ref[0]
    for peer in range(1, in_ref.shape[0]):
        value = value + in_ref[peer]
    solved = eliminate(jnp.concatenate([side_ref[:, 0:R] * value[:, 0:R], value[:, R : 2 * R]], axis=1))
    out_ref[...] = solved[:, R : R + KD].T


def vmem(count):
    return [pl.BlockSpec(memory_space=pltpu.VMEM)] * count


def params():
    return pltpu.CompilerParams(vmem_limit_bytes=48 * 1024 * 1024)


def f32(*shape):
    return jax.ShapeDtypeStruct(shape, jnp.float32)


def exchange(value, axes):
    return lax.all_to_all(value, axes, 0, 0, tiled=True)


def share(value, axes, peers):
    return exchange(jnp.broadcast_to(value[None], (peers,) + value.shape), axes)


def body(sizes, series, lengths, tile_owner, factor_h, factor_v, weights_s):
    ny, nz, nc, nx = sizes
    rows, width = series.shape
    slots = tile_owner.shape[0]
    quarter = rows // nx
    w_rows = weights_s.T
    parts = pl.pallas_call(
        partial_kernel,
        grid=(nx,),
        in_specs=[
            pl.BlockSpec((R, width), lambda i: (0, 0)),
            pl.BlockSpec((quarter, width), lambda i: (i, 0)),
        ],
        out_specs=pl.BlockSpec((1, R, quarter), lambda i: (i, 0, 0)),
        out_shape=jax.ShapeDtypeStruct((nx, R, quarter), jnp.bfloat16),
        compiler_params=params(),
    )(factor_v, series)
    parts = jnp.sum(exchange(parts, "x").astype(jnp.float32), axis=0).astype(jnp.bfloat16)
    parts = share(parts, "x", nx)
    proj, pack = pl.pallas_call(
        functools.partial(polar_kernel, peers=nx, spread=ny * nz * nc),
        in_specs=[pl.BlockSpec(memory_space=pltpu.SMEM)] * 2 + vmem(5),
        out_specs=vmem(2),
        out_shape=[f32(R, KD * width), f32(2 * R, 2 * R)],
        scratch_shapes=[
            pltpu.VMEM((R, rows), jnp.bfloat16),
            pltpu.VMEM((KD + 1, R, R), jnp.float32),
            pltpu.VMEM((KD + 1, 3, R, R), jnp.bfloat16),
            pltpu.VMEM((KD + 1, R, width), jnp.float32),
        ],
        compiler_params=params(),
    )(tile_owner, lengths, parts, series, factor_h, factor_v, w_rows)
    near = ny * nc * nx
    pieces = exchange(pack.reshape(near, 2 * R // near, 2 * R), ("y", "c", "x"))
    pieces = share(jnp.sum(pieces, axis=0), "z", nz)
    pieces = share(jnp.sum(pieces, axis=0), ("y", "c", "x"), near)
    new_h, hp, col, side = pl.pallas_call(
        head_kernel,
        in_specs=vmem(3),
        out_specs=vmem(4),
        out_shape=[f32(R, R), f32(R, KD * width), f32(R * width // TILE, TILE), f32(R, 2 * R)],
        compiler_params=params(),
    )(pieces.reshape(2 * R, 2 * R), proj, w_rows)
    near = ny * nc
    pieces = exchange(col.reshape(near, col.shape[0] // near, TILE), ("y", "c"))
    pieces = share(jnp.sum(pieces, axis=0).astype(jnp.bfloat16), "z", nz).astype(jnp.float32)
    pieces = share(jnp.sum(pieces, axis=0), ("y", "c"), near)
    new_v, sums = pl.pallas_call(
        column_kernel,
        in_specs=vmem(3),
        out_specs=vmem(2),
        out_shape=[f32(R, width), f32(nx, R, 2 * R)],
        compiler_params=params(),
    )(pieces.reshape(col.shape), hp, side)
    new_s = pl.pallas_call(
        weight_kernel,
        in_specs=vmem(2),
        out_specs=pl.BlockSpec(memory_space=pltpu.VMEM),
        out_shape=f32(KD, R),
        compiler_params=params(),
    )(exchange(sums, "x"), side)
    return (new_h, new_v, new_s.T)


def solution(mesh):
    traj, nx = mesh.devices.shape
    ny, nc = (4, 2) if traj % 128 == 0 else (2, 2)
    sizes = (ny, traj // (ny * nc), nc, nx)
    fine = Mesh(mesh.devices.reshape(sizes), ("y", "z", "c", "x"))
    traj_axes = ("y", "z", "c")
    return jax.shard_map(
        functools.partial(body, sizes),
        mesh=fine,
        in_specs=(P(traj_axes, "x"), P(traj_axes), P(traj_axes), P(), P(None, "x"), P(None, traj_axes)),
        out_specs=(P(), P(None, "x"), P(None, traj_axes)),
        check_vma=False,
    )
```

```python
import functools

import jax
import jax.numpy as jnp
from jax import lax
from jax.experimental import pallas as pl
from jax.experimental.pallas import tpu as pltpu
from jax.sharding import Mesh, PartitionSpec as P

ITERS = 8
R = 64
TILE = 128
KD = 4
LANES = (((1,), (1,)), ((), ()))

highest = lax.Precision.HIGHEST


def mm(left, right):
    return jnp.dot(left, right, precision=highest, preferred_element_type=jnp.float32)


def mm_t(left, right):
    return lax.dot_general(left, right, LANES, precision=highest, preferred_element_type=jnp.float32)


def halves(value):
    high = value.astype(jnp.bfloat16)
    return high, (value - high.astype(jnp.float32)).astype(jnp.bfloat16)


def mm_halves(left, right, dims=(((1,), (0,)), ((), ()))):
    rows, cols = left.shape[0], right.shape[1 - dims[0][1][0]]
    left = jnp.concatenate(halves(left), axis=0)
    right = jnp.concatenate(halves(right), axis=1 - dims[0][1][0])
    terms = lax.dot_general(left, right, dims, preferred_element_type=jnp.float32)
    return terms[0:rows, 0:cols] + (terms[0:rows, cols:] + terms[rows:, 0:cols])


def eye_mask():
    rows = lax.broadcasted_iota(jnp.int32, (R, R), 0)
    cols = lax.broadcasted_iota(jnp.int32, (R, R), 1)
    return rows == cols


def eliminate(both):
    rows = lax.broadcasted_iota(jnp.int32, both.shape, 0)
    for k in range(0, R, 4):
        col = [jnp.broadcast_to(both[:, k + i : k + i + 1], both.shape) for i in range(4)]
        row = [both[k + i : k + i + 1, :] for i in range(4)]
        piv = [[col[j][k + i : k + i + 1, :] for j in range(4)] for i in range(4)]
        inv = 1.0 / (piv[0][0] * piv[1][1] - piv[0][1] * piv[0][1])
        a00, a01, a11 = piv[1][1] * inv, -piv[0][1] * inv, piv[0][0] * inv
        e02, e12 = a00 * piv[0][2] + a01 * piv[1][2], a01 * piv[0][2] + a11 * piv[1][2]
        e03, e13 = a00 * piv[0][3] + a01 * piv[1][3], a01 * piv[0][3] + a11 * piv[1][3]
        s22 = piv[2][2] - (piv[0][2] * e02 + piv[1][2] * e12)
        s23 = piv[2][3] - (piv[0][2] * e03 + piv[1][2] * e13)
        s33 = piv[3][3] - (piv[0][3] * e03 + piv[1][3] * e13)
        inv = 1.0 / (s22 * s33 - s23 * s23)
        t2 = row[2] - e02 * row[0] - e12 * row[1]
        t3 = row[3] - e03 * row[0] - e13 * row[1]
        n2, n3 = (s33 * t2 - s23 * t3) * inv, (s22 * t3 - s23 * t2) * inv
        n0 = (a00 * row[0] + a01 * row[1]) - e02 * n2 - e03 * n3
        n1 = (a01 * row[0] + a11 * row[1]) - e12 * n2 - e13 * n3
        rest = (both - col[0] * n0 - col[1] * n1) - (col[2] * n2 + col[3] * n3)
        for i, new in enumerate((n0, n1, n2, n3)):
            rest = jnp.where(rows == k + i, new, rest)
        both = rest
    return both


def partial_kernel(v_ref, s_ref, out_ref, v_buf, s_buf, sems):
    count, _, quarter = out_ref.shape
    pieces = 2
    step = count * quarter // pieces
    copies = [pltpu.make_async_copy(v_ref, v_buf, sems.at[pieces])]
    for i in range(pieces):
        rows = pl.ds(i * step, step)
        copies.append(pltpu.make_async_copy(s_ref.at[rows, :], s_buf.at[rows, :], sems.at[i]))
    for copy in copies:
        copy.start()
    copies[0].wait()
    factor_bf = v_buf[...].astype(jnp.bfloat16)
    for i in range(pieces):
        copies[i + 1].wait()
        for peer in range(i * count // pieces, max((i + 1) * count // pieces, i * count // pieces + 1)):
            out_ref[peer] = lax.dot_general(
                factor_bf, s_buf[peer * quarter : (peer + 1) * quarter, :], LANES, preferred_element_type=jnp.float32
            ).astype(jnp.bfloat16)


def three(value):
    high = value.astype(jnp.bfloat16)
    rest = value - high.astype(jnp.float32)
    middle = rest.astype(jnp.bfloat16)
    return high, middle, (rest - middle.astype(jnp.float32)).astype(jnp.bfloat16)


def polar_kernel(
    owner_ref, length_ref, part_ref, s_ref, h_ref, v_ref, w_ref, proj_ref, pack_ref, p_ref, *, peers, spread
):
    rows, width = s_ref.shape
    slots = rows // TILE
    eye = eye_mask()
    lane = lax.broadcasted_iota(jnp.int32, (1, rows), 1)
    masks = []
    for k in range(KD):
        first = jnp.int32(0)
        for t in range(slots if k > 0 else 0):
            first = first + jnp.where(owner_ref[t] < k, TILE, 0)
        live = (lane >= first) & (lane < first + length_ref[k])
        masks.append(jnp.where(live, 1.0, 0.0).astype(jnp.bfloat16))
    summed = jnp.concatenate([part_ref[peer] for peer in range(peers)], axis=1)
    for k in range(KD):
        p_ref[k * R : (k + 1) * R, :] = summed * masks[k]
    products = lax.dot_general(summed, p_ref[...], LANES, preferred_element_type=jnp.float32)
    hmat = h_ref[...]
    wmat = w_ref[...].T
    wide_eye = jnp.where(
        lax.broadcasted_iota(jnp.int32, (R, 2 * R), 0) == lax.broadcasted_iota(jnp.int32, (R, 2 * R), 1), 1.5, 0.0
    )
    both = []
    for k in range(KD):
        mix = hmat * jnp.sum(jnp.where(eye, wmat[:, k : k + 1], 0.0), axis=0, keepdims=True)
        gram = mm_t(mm(mix, products[:, k * R : (k + 1) * R]), mix)
        energy = jnp.sum(jnp.where(eye, gram, 0.0), keepdims=True)
        scale = lax.rsqrt(energy + 1e-06)
        both.append(jnp.concatenate([gram * (scale * scale), mix * scale], axis=1))
    for iteration in range(ITERS):
        steps = [wide_eye - 0.5 * pair for pair in both]
        both = [mm_halves(step[:, 0:R], pair) for step, pair in zip(steps, both)]
        if iteration < ITERS - 1:
            next_grams = [mm_halves(pair[:, 0:R], step) for step, pair in zip(steps, both)]
            first_half = lax.broadcasted_iota(jnp.int32, (R, 2 * R), 1) < R
            both = [jnp.where(first_half, gram, pair) for gram, pair in zip(next_grams, both)]
    parts = [three(pair[:, R : 2 * R]) for pair in both]
    turn_rows = jnp.concatenate(
        [jnp.concatenate([parts[k][i] for k in range(KD)], axis=1) for i in range(3)], axis=0
    )
    chunk = 2 * TILE
    for first in range(0, rows, chunk):
        cols = slice(first, first + chunk)
        terms = jnp.dot(turn_rows, p_ref[:, cols], preferred_element_type=jnp.float32)
        polar = (terms[0:R] + (terms[R : 2 * R] + terms[2 * R : 3 * R])).astype(jnp.bfloat16)
        for k in range(KD):
            p_ref[k * R : (k + 1) * R, cols] = polar * masks[k][:, cols]
    projected = jnp.dot(p_ref[...], s_ref[...], preferred_element_type=jnp.float32)
    vmat = v_ref[...]
    head = jnp.zeros((R, R), jnp.float32)
    for k in range(KD):
        block = projected[k * R : (k + 1) * R, :]
        proj_ref[:, k * width : (k + 1) * width] = block
        head = head + mm_halves(block, vmat * wmat[:, k : k + 1], LANES)
    pack_ref[0:R, :] = jnp.concatenate([head, mm_t(wmat, wmat) * (1.0 / peers)], axis=1)
    pack_ref[R : 2 * R, :] = jnp.concatenate(
        [mm_t(vmat, vmat) * (1.0 / spread), jnp.zeros((R, R), jnp.float32)], axis=1
    )


def head_kernel(pack_ref, proj_ref, w_ref, newh_ref, hp_ref, col_ref, side_ref):
    head, wgram = pack_ref[0:R, 0:R], pack_ref[0:R, R : 2 * R]
    fgram = pack_ref[R : 2 * R, 0:R]
    newh_t = eliminate(jnp.concatenate([fgram * wgram, head.T], axis=1))[:, R:]
    newh_ref[...] = newh_t.T
    wmat = w_ref[...].T
    hp = mm_halves(newh_t, proj_ref[...])
    hp_ref[...] = hp
    width = hp.shape[1] // KD
    col = hp[:, 0:width] * wmat[:, 0:1]
    for k in range(1, KD):
        col = col + hp[:, k * width : (k + 1) * width] * wmat[:, k : k + 1]
    for half in range(width // TILE):
        col_ref[half * R : (half + 1) * R, :] = col[:, half * TILE : (half + 1) * TILE]
    hgram = mm_t(newh_t, newh_t)
    inverse = eliminate(jnp.concatenate([hgram * wgram, jnp.where(eye_mask(), 1.0, 0.0)], axis=1))[:, R:]
    side_ref[...] = jnp.concatenate([hgram, inverse], axis=1)


def column_kernel(col_ref, hp_ref, inverse_ref, newv_ref, out_ref):
    halves = col_ref.shape[0] // R
    col = jnp.concatenate([col_ref[half * R : (half + 1) * R, :] for half in range(halves)], axis=1)
    newv = mm(inverse_ref[:, R : 2 * R], col)
    newv_ref[...] = newv
    width = newv.shape[1]
    lane = lax.broadcasted_iota(jnp.int32, (R, R), 1)
    terms = jnp.zeros((R, R), jnp.float32)
    for k in range(KD):
        sums = jnp.sum(hp_ref[:, k * width : (k + 1) * width] * newv, axis=1, keepdims=True)
        terms = jnp.where(lane == k, sums, terms)
    value = jnp.concatenate([mm_t(newv, newv), terms], axis=1)
    for peer in range(out_ref.shape[0]):
        out_ref[peer] = value


def weight_kernel(in_ref, side_ref, out_ref):
    value = in_ref[0]
    for peer in range(1, in_ref.shape[0]):
        value = value + in_ref[peer]
    solved = eliminate(jnp.concatenate([side_ref[:, 0:R] * value[:, 0:R], value[:, R : 2 * R]], axis=1))
    out_ref[...] = solved[:, R : R + KD].T


def vmem(count):
    return [pl.BlockSpec(memory_space=pltpu.VMEM)] * count


def params(mib=48):
    return pltpu.CompilerParams(vmem_limit_bytes=mib * 1024 * 1024)


def f32(*shape):
    return jax.ShapeDtypeStruct(shape, jnp.float32)


def exchange(value, axes):
    return lax.all_to_all(value, axes, 0, 0, tiled=True)


def share(value, axes, peers):
    return exchange(jnp.broadcast_to(value[None], (peers,) + value.shape), axes)


def body(sizes, series, lengths, tile_owner, factor_h, factor_v, weights_s):
    ny, nz, nc, nx = sizes
    rows, width = series.shape
    slots = tile_owner.shape[0]
    quarter = rows // nx
    w_rows = weights_s.T
    parts = pl.pallas_call(
        partial_kernel,
        in_specs=[pl.BlockSpec(memory_space=pltpu.HBM)] * 2,
        out_specs=pl.BlockSpec(memory_space=pltpu.VMEM),
        out_shape=jax.ShapeDtypeStruct((nx, R, quarter), jnp.bfloat16),
        scratch_shapes=[
            pltpu.VMEM((R, width), jnp.float32),
            pltpu.VMEM((rows, width), jnp.bfloat16),
            pltpu.SemaphoreType.DMA((nx + 1,)),
        ],
        compiler_params=params(63),
    )(factor_v, series)
    parts = jnp.sum(exchange(parts, "x").astype(jnp.float32), axis=0).astype(jnp.bfloat16)
    parts = share(parts, "x", nx)
    proj, pack = pl.pallas_call(
        functools.partial(polar_kernel, peers=nx, spread=ny * nz * nc),
        in_specs=[pl.BlockSpec(memory_space=pltpu.SMEM)] * 2 + vmem(5),
        out_specs=vmem(2),
        out_shape=[f32(R, KD * width), f32(2 * R, 2 * R)],
        scratch_shapes=[
            pltpu.VMEM((KD * R, rows), jnp.bfloat16),
        ],
        compiler_params=params(),
    )(tile_owner, lengths, parts, series, factor_h, factor_v, w_rows)
    near = ny * nc * nx
    pieces = exchange(pack.reshape(near, 2 * R // near, 2 * R), ("y", "c", "x"))
    pieces = share(jnp.sum(pieces, axis=0), "z", nz)
    pieces = share(jnp.sum(pieces, axis=0), ("y", "c", "x"), near)
    new_h, hp, col, side = pl.pallas_call(
        head_kernel,
        in_specs=vmem(3),
        out_specs=vmem(4),
        out_shape=[f32(R, R), f32(R, KD * width), f32(R * width // TILE, TILE), f32(R, 2 * R)],
        compiler_params=params(),
    )(pieces.reshape(2 * R, 2 * R), proj, w_rows)
    near = ny * nc
    pieces = exchange(col.reshape(near, col.shape[0] // near, TILE), ("y", "c"))
    pieces = share(jnp.sum(pieces, axis=0).astype(jnp.bfloat16), "z", nz).astype(jnp.float32)
    pieces = share(jnp.sum(pieces, axis=0), ("y", "c"), near)
    new_v, sums = pl.pallas_call(
        column_kernel,
        in_specs=vmem(3),
        out_specs=vmem(2),
        out_shape=[f32(R, width), f32(nx, R, 2 * R)],
        compiler_params=params(),
    )(pieces.reshape(col.shape), hp, side)
    new_s = pl.pallas_call(
        weight_kernel,
        in_specs=vmem(2),
        out_specs=pl.BlockSpec(memory_space=pltpu.VMEM),
        out_shape=f32(KD, R),
        compiler_params=params(),
    )(exchange(sums, "x"), side)
    return (new_h, new_v, new_s.T)


def solution(mesh):
    traj, nx = mesh.devices.shape
    ny, nc = (4, 2) if traj % 128 == 0 else (2, 2)
    sizes = (ny, traj // (ny * nc), nc, nx)
    fine = Mesh(mesh.devices.reshape(sizes), ("y", "z", "c", "x"))
    traj_axes = ("y", "z", "c")
    return jax.shard_map(
        functools.partial(body, sizes),
        mesh=fine,
        in_specs=(P(traj_axes, "x"), P(traj_axes), P(traj_axes), P(), P(None, "x"), P(None, traj_axes)),
        out_specs=(P(), P(None, "x"), P(None, traj_axes)),
        check_vma=False,
    )
```

```python
import functools

import jax
import jax.numpy as jnp
from jax import lax
from jax.experimental import pallas as pl
from jax.experimental.pallas import tpu as pltpu
from jax.sharding import Mesh, PartitionSpec as P

ITERS = 8
R = 64
TILE = 128
KD = 4
LANES = (((1,), (1,)), ((), ()))

highest = lax.Precision.HIGHEST


def mm(left, right):
    return jnp.dot(left, right, precision=highest, preferred_element_type=jnp.float32)


def mm_t(left, right):
    return lax.dot_general(left, right, LANES, precision=highest, preferred_element_type=jnp.float32)


def halves(value):
    high = value.astype(jnp.bfloat16)
    return high, (value - high.astype(jnp.float32)).astype(jnp.bfloat16)


def mm_halves(left, right, dims=(((1,), (0,)), ((), ()))):
    rows, cols = left.shape[0], right.shape[1 - dims[0][1][0]]
    left = jnp.concatenate(halves(left), axis=0)
    right = jnp.concatenate(halves(right), axis=1 - dims[0][1][0])
    terms = lax.dot_general(left, right, dims, preferred_element_type=jnp.float32)
    return terms[0:rows, 0:cols] + (terms[0:rows, cols:] + terms[rows:, 0:cols])


def eye_mask():
    rows = lax.broadcasted_iota(jnp.int32, (R, R), 0)
    cols = lax.broadcasted_iota(jnp.int32, (R, R), 1)
    return rows == cols


def eliminate(both, block=8):
    rows = lax.broadcasted_iota(jnp.int32, both.shape, 0)
    for k in range(0, R, block):
        col = [jnp.broadcast_to(both[:, k + i : k + i + 1], both.shape) for i in range(block)]
        row = [both[k + i : k + i + 1, :] for i in range(block)]
        piv = [[col[j][k + i : k + i + 1, :] for j in range(block)] for i in range(block)]
        for q in range(0, block, 2):
            inv = 1.0 / (piv[q][q] * piv[q + 1][q + 1] - piv[q][q + 1] * piv[q + 1][q])
            a00, a01 = piv[q + 1][q + 1] * inv, -piv[q][q + 1] * inv
            a10, a11 = -piv[q + 1][q] * inv, piv[q][q] * inv
            new0, new1 = a00 * row[q] + a01 * row[q + 1], a10 * row[q] + a11 * row[q + 1]
            later = range(q + 2, block)
            solved = {
                j: (a00 * piv[q][j] + a01 * piv[q + 1][j], a10 * piv[q][j] + a11 * piv[q + 1][j])
                for j in later
            }
            for i in range(block):
                if i in (q, q + 1):
                    continue
                row[i] = row[i] - (piv[i][q] * new0 + piv[i][q + 1] * new1)
                for j in later:
                    piv[i][j] = piv[i][j] - (piv[i][q] * solved[j][0] + piv[i][q + 1] * solved[j][1])
            row[q], row[q + 1] = new0, new1
            for j in later:
                piv[q][j], piv[q + 1][j] = solved[j]
        rest = both
        for i in range(0, block, 2):
            rest = rest - (col[i] * row[i] + col[i + 1] * row[i + 1])
        for i in range(block):
            rest = jnp.where(rows == k + i, row[i], rest)
        both = rest
    return both


def partial_kernel(v_ref, s_ref, out_ref, v_buf, s_buf, sems):
    count, _, quarter = out_ref.shape
    pieces = 2
    step = count * quarter // pieces
    copies = [pltpu.make_async_copy(v_ref, v_buf, sems.at[pieces])]
    for i in range(pieces):
        rows = pl.ds(i * step, step)
        copies.append(pltpu.make_async_copy(s_ref.at[rows, :], s_buf.at[rows, :], sems.at[i]))
    for copy in copies:
        copy.start()
    copies[0].wait()
    factor_bf = v_buf[...].astype(jnp.bfloat16)
    for i in range(pieces):
        copies[i + 1].wait()
        for peer in range(i * count // pieces, max((i + 1) * count // pieces, i * count // pieces + 1)):
            out_ref[peer] = lax.dot_general(
                factor_bf, s_buf[peer * quarter : (peer + 1) * quarter, :], LANES, preferred_element_type=jnp.float32
            ).astype(jnp.bfloat16)


def three(value):
    high = value.astype(jnp.bfloat16)
    rest = value - high.astype(jnp.float32)
    middle = rest.astype(jnp.bfloat16)
    return high, middle, (rest - middle.astype(jnp.float32)).astype(jnp.bfloat16)


def polar_kernel(
    owner_ref, length_ref, part_ref, s_ref, h_ref, v_ref, w_ref, proj_ref, pack_ref, p_ref, *, peers, spread
):
    rows, width = s_ref.shape
    slots = rows // TILE
    eye = eye_mask()
    lane = lax.broadcasted_iota(jnp.int32, (1, rows), 1)
    masks = []
    for k in range(KD):
        first = jnp.int32(0)
        for t in range(slots if k > 0 else 0):
            first = first + jnp.where(owner_ref[t] < k, TILE, 0)
        live = (lane >= first) & (lane < first + length_ref[k])
        masks.append(jnp.where(live, 1.0, 0.0).astype(jnp.bfloat16))
    summed = jnp.concatenate([part_ref[peer] for peer in range(peers)], axis=1)
    for k in range(KD):
        p_ref[k * R : (k + 1) * R, :] = summed * masks[k]
    hmat = h_ref[...]
    wmat = w_ref[...].T
    hgram = lax.dot_general(
        hmat, hmat, (((0,), (0,)), ((), ())), precision=highest, preferred_element_type=jnp.float32
    )
    products = lax.dot_general(summed, p_ref[...], LANES, preferred_element_type=jnp.float32)
    wide_eye = jnp.where(
        lax.broadcasted_iota(jnp.int32, (R, 2 * R), 0) == lax.broadcasted_iota(jnp.int32, (R, 2 * R), 1), 1.5, 0.0
    )
    column_rows = [
        jnp.sum(jnp.where(eye, wmat[:, k : k + 1], 0.0), axis=0, keepdims=True) for k in range(KD)
    ]
    both = []
    for k in range(KD):
        column = wmat[:, k : k + 1]
        mix = hmat * column_rows[k]
        product = products[:, k * R : (k + 1) * R]
        gram = mm_t(mm(mix, product), mix)
        energy = jnp.sum(product * (hgram * column * column_rows[k]), keepdims=True)
        scale = lax.rsqrt(energy + 1e-06)
        both.append(jnp.concatenate([gram * (scale * scale), mix * scale], axis=1))
    for iteration in range(ITERS):
        steps = [wide_eye - 0.5 * pair for pair in both]
        both = [mm_halves(step[:, 0:R], pair) for step, pair in zip(steps, both)]
        if iteration < ITERS - 1:
            next_grams = [mm_halves(pair[:, 0:R], step) for step, pair in zip(steps, both)]
            first_half = lax.broadcasted_iota(jnp.int32, (R, 2 * R), 1) < R
            both = [jnp.where(first_half, gram, pair) for gram, pair in zip(next_grams, both)]
    parts = [three(pair[:, R : 2 * R]) for pair in both]
    turn_rows = jnp.concatenate(
        [jnp.concatenate([parts[k][i] for k in range(KD)], axis=1) for i in range(3)], axis=0
    )
    chunk = 2 * TILE
    for first in range(0, rows, chunk):
        cols = slice(first, first + chunk)
        terms = jnp.dot(turn_rows, p_ref[:, cols], preferred_element_type=jnp.float32)
        polar = (terms[0:R] + (terms[R : 2 * R] + terms[2 * R : 3 * R])).astype(jnp.bfloat16)
        for k in range(KD):
            p_ref[k * R : (k + 1) * R, cols] = polar * masks[k][:, cols]
    projected = jnp.dot(p_ref[...], s_ref[...], preferred_element_type=jnp.float32)
    vmat = v_ref[...]
    head = jnp.zeros((R, R), jnp.float32)
    for k in range(KD):
        block = projected[k * R : (k + 1) * R, :]
        proj_ref[:, k * width : (k + 1) * width] = block
        head = head + mm_halves(block, vmat * wmat[:, k : k + 1], LANES)
    pack_ref[0:R, :] = jnp.concatenate([head, mm_t(wmat, wmat) * (1.0 / peers)], axis=1)
    pack_ref[R : 2 * R, :] = jnp.concatenate(
        [mm_t(vmat, vmat) * (1.0 / spread), jnp.zeros((R, R), jnp.float32)], axis=1
    )


def head_kernel(pack_ref, proj_ref, w_ref, newh_ref, hp_ref, col_ref, side_ref):
    head, wgram = pack_ref[0:R, 0:R], pack_ref[0:R, R : 2 * R]
    fgram = pack_ref[R : 2 * R, 0:R]
    newh_t = eliminate(jnp.concatenate([fgram * wgram, head.T], axis=1))[:, R:]
    newh_ref[...] = newh_t.T
    wmat = w_ref[...].T
    hp = mm_halves(newh_t, proj_ref[...])
    hp_ref[...] = hp
    width = hp.shape[1] // KD
    col = hp[:, 0:width] * wmat[:, 0:1]
    for k in range(1, KD):
        col = col + hp[:, k * width : (k + 1) * width] * wmat[:, k : k + 1]
    for half in range(width // TILE):
        col_ref[half * R : (half + 1) * R, :] = col[:, half * TILE : (half + 1) * TILE].astype(jnp.bfloat16)
    hgram = mm_t(newh_t, newh_t)
    inverse = eliminate(jnp.concatenate([hgram * wgram, jnp.where(eye_mask(), 1.0, 0.0)], axis=1))[:, R:]
    side_ref[...] = jnp.concatenate([hgram, inverse], axis=1)


def column_kernel(col_ref, hp_ref, inverse_ref, newv_ref, out_ref):
    halves = col_ref.shape[0] // R
    col = jnp.concatenate([col_ref[half * R : (half + 1) * R, :] for half in range(halves)], axis=1)
    newv = mm(inverse_ref[:, R : 2 * R], col)
    newv_ref[...] = newv
    width = newv.shape[1]
    lane = lax.broadcasted_iota(jnp.int32, (R, R), 1)
    terms = jnp.zeros((R, R), jnp.float32)
    for k in range(KD):
        sums = jnp.sum(hp_ref[:, k * width : (k + 1) * width] * newv, axis=1, keepdims=True)
        terms = jnp.where(lane == k, sums, terms)
    value = jnp.concatenate([mm_t(newv, newv), terms], axis=1)
    for peer in range(out_ref.shape[0]):
        out_ref[peer] = value


def weight_kernel(in_ref, side_ref, out_ref):
    value = in_ref[0]
    for peer in range(1, in_ref.shape[0]):
        value = value + in_ref[peer]
    solved = eliminate(jnp.concatenate([side_ref[:, 0:R] * value[:, 0:R], value[:, R : 2 * R]], axis=1))
    out_ref[...] = solved[:, R : R + KD].T


def vmem(count):
    return [pl.BlockSpec(memory_space=pltpu.VMEM)] * count


def params(mib=48):
    return pltpu.CompilerParams(vmem_limit_bytes=mib * 1024 * 1024)


def f32(*shape):
    return jax.ShapeDtypeStruct(shape, jnp.float32)


def exchange(value, axes):
    return lax.all_to_all(value, axes, 0, 0, tiled=True)


def share(value, axes, peers):
    return exchange(jnp.broadcast_to(value[None], (peers,) + value.shape), axes)


def body(sizes, series, lengths, tile_owner, factor_h, factor_v, weights_s):
    ny, nz, nc, nx = sizes
    rows, width = series.shape
    slots = tile_owner.shape[0]
    quarter = rows // nx
    w_rows = weights_s.T
    parts = pl.pallas_call(
        partial_kernel,
        in_specs=[pl.BlockSpec(memory_space=pltpu.HBM)] * 2,
        out_specs=pl.BlockSpec(memory_space=pltpu.VMEM),
        out_shape=jax.ShapeDtypeStruct((nx, R, quarter), jnp.bfloat16),
        scratch_shapes=[
            pltpu.VMEM((R, width), jnp.float32),
            pltpu.VMEM((rows, width), jnp.bfloat16),
            pltpu.SemaphoreType.DMA((nx + 1,)),
        ],
        compiler_params=params(63),
    )(factor_v, series)
    parts = jnp.sum(exchange(parts, "x").astype(jnp.float32), axis=0).astype(jnp.bfloat16)
    parts = share(parts, "x", nx)
    proj, pack = pl.pallas_call(
        functools.partial(polar_kernel, peers=nx, spread=ny * nz * nc),
        in_specs=[pl.BlockSpec(memory_space=pltpu.SMEM)] * 2 + vmem(5),
        out_specs=vmem(2),
        out_shape=[f32(R, KD * width), f32(2 * R, 2 * R)],
        scratch_shapes=[
            pltpu.VMEM((KD * R, rows), jnp.bfloat16),
        ],
        compiler_params=params(),
    )(tile_owner, lengths, parts, series, factor_h, factor_v, w_rows)
    near = ny * nc * nx
    pieces = exchange(pack.reshape(near, 2 * R // near, 2 * R), ("y", "c", "x"))
    pieces = share(jnp.sum(pieces, axis=0), "z", nz)
    pieces = share(jnp.sum(pieces, axis=0), ("y", "c", "x"), near)
    new_h, hp, col, side = pl.pallas_call(
        head_kernel,
        in_specs=vmem(3),
        out_specs=vmem(4),
        out_shape=[f32(R, R), f32(R, KD * width), jax.ShapeDtypeStruct((R * width // TILE, TILE), jnp.bfloat16), f32(R, 2 * R)],
        compiler_params=params(),
    )(pieces.reshape(2 * R, 2 * R), proj, w_rows)
    near = ny * nc
    pieces = exchange(col.reshape(near, col.shape[0] // near, TILE), ("y", "c"))
    pieces = share(jnp.sum(pieces.astype(jnp.float32), axis=0).astype(jnp.bfloat16), "z", nz).astype(jnp.float32)
    pieces = share(jnp.sum(pieces, axis=0), ("y", "c"), near)
    new_v, sums = pl.pallas_call(
        column_kernel,
        in_specs=vmem(3),
        out_specs=vmem(2),
        out_shape=[f32(R, width), f32(nx, R, 2 * R)],
        compiler_params=params(),
    )(pieces.reshape(col.shape), hp, side)
    new_s = pl.pallas_call(
        weight_kernel,
        in_specs=vmem(2),
        out_specs=pl.BlockSpec(memory_space=pltpu.VMEM),
        out_shape=f32(KD, R),
        compiler_params=params(),
    )(exchange(sums, "x"), side)
    return (new_h, new_v, new_s.T)


def solution(mesh):
    traj, nx = mesh.devices.shape
    ny, nc = (4, 2) if traj % 128 == 0 else (2, 2)
    sizes = (ny, traj // (ny * nc), nc, nx)
    fine = Mesh(mesh.devices.reshape(sizes), ("y", "z", "c", "x"))
    traj_axes = ("y", "z", "c")
    return jax.shard_map(
        functools.partial(body, sizes),
        mesh=fine,
        in_specs=(P(traj_axes, "x"), P(traj_axes), P(traj_axes), P(), P(None, "x"), P(None, traj_axes)),
        out_specs=(P(), P(None, "x"), P(None, traj_axes)),
        check_vma=False,
    )
```

```python
import functools

import jax
import jax.numpy as jnp
from jax import lax
from jax.experimental import pallas as pl
from jax.experimental.pallas import tpu as pltpu
from jax.sharding import Mesh, PartitionSpec as P

ITERS = 8
R = 64
TILE = 128
KD = 4
LANES = (((1,), (1,)), ((), ()))

highest = lax.Precision.HIGHEST


def mm(left, right):
    return jnp.dot(left, right, precision=highest, preferred_element_type=jnp.float32)


def mm_t(left, right):
    return lax.dot_general(left, right, LANES, precision=highest, preferred_element_type=jnp.float32)


def halves(value):
    high = value.astype(jnp.bfloat16)
    return high, (value - high.astype(jnp.float32)).astype(jnp.bfloat16)


def mm_halves(left, right, dims=(((1,), (0,)), ((), ()))):
    rows, cols = left.shape[0], right.shape[1 - dims[0][1][0]]
    left = jnp.concatenate(halves(left), axis=0)
    right = jnp.concatenate(halves(right), axis=1 - dims[0][1][0])
    terms = lax.dot_general(left, right, dims, preferred_element_type=jnp.float32)
    return terms[0:rows, 0:cols] + (terms[0:rows, cols:] + terms[rows:, 0:cols])


def eye_mask():
    rows = lax.broadcasted_iota(jnp.int32, (R, R), 0)
    cols = lax.broadcasted_iota(jnp.int32, (R, R), 1)
    return rows == cols


def eliminate(both, block=8):
    rows = lax.broadcasted_iota(jnp.int32, both.shape, 0)
    for k in range(0, R, block):
        col = [jnp.broadcast_to(both[:, k + i : k + i + 1], both.shape) for i in range(block)]
        row = [both[k + i : k + i + 1, :] for i in range(block)]
        piv = [[col[j][k + i : k + i + 1, :] for j in range(block)] for i in range(block)]
        for q in range(0, block, 2):
            inv = 1.0 / (piv[q][q] * piv[q + 1][q + 1] - piv[q][q + 1] * piv[q + 1][q])
            a00, a01 = piv[q + 1][q + 1] * inv, -piv[q][q + 1] * inv
            a10, a11 = -piv[q + 1][q] * inv, piv[q][q] * inv
            new0, new1 = a00 * row[q] + a01 * row[q + 1], a10 * row[q] + a11 * row[q + 1]
            later = range(q + 2, block)
            solved = {
                j: (a00 * piv[q][j] + a01 * piv[q + 1][j], a10 * piv[q][j] + a11 * piv[q + 1][j])
                for j in later
            }
            for i in range(block):
                if i in (q, q + 1):
                    continue
                row[i] = row[i] - (piv[i][q] * new0 + piv[i][q + 1] * new1)
                for j in later:
                    piv[i][j] = piv[i][j] - (piv[i][q] * solved[j][0] + piv[i][q + 1] * solved[j][1])
            row[q], row[q + 1] = new0, new1
            for j in later:
                piv[q][j], piv[q + 1][j] = solved[j]
        rest = both
        for i in range(0, block, 2):
            rest = rest - (col[i] * row[i] + col[i + 1] * row[i + 1])
        for i in range(block):
            rest = jnp.where(rows == k + i, row[i], rest)
        both = rest
    return both


def partial_kernel(v_ref, s_ref, out_ref, v_buf, s_buf, sems):
    count, _, quarter = out_ref.shape
    pieces = 2
    step = count * quarter // pieces
    copies = [pltpu.make_async_copy(v_ref, v_buf, sems.at[pieces])]
    for i in range(pieces):
        rows = pl.ds(i * step, step)
        copies.append(pltpu.make_async_copy(s_ref.at[rows, :], s_buf.at[rows, :], sems.at[i]))
    for copy in copies:
        copy.start()
    copies[0].wait()
    factor_bf = v_buf[...].astype(jnp.bfloat16)
    for i in range(pieces):
        copies[i + 1].wait()
        for peer in range(i * count // pieces, max((i + 1) * count // pieces, i * count // pieces + 1)):
            out_ref[peer] = lax.dot_general(
                factor_bf, s_buf[peer * quarter : (peer + 1) * quarter, :], LANES, preferred_element_type=jnp.float32
            ).astype(jnp.bfloat16)


def three(value):
    high = value.astype(jnp.bfloat16)
    rest = value - high.astype(jnp.float32)
    middle = rest.astype(jnp.bfloat16)
    return high, middle, (rest - middle.astype(jnp.float32)).astype(jnp.bfloat16)


def polar_kernel(
    owner_ref, length_ref, part_ref, s_ref, h_ref, v_ref, w_ref, proj_ref, send_ref, p_ref, *, peers
):
    rows, width = s_ref.shape
    slots = rows // TILE
    eye = eye_mask()
    lane = lax.broadcasted_iota(jnp.int32, (1, rows), 1)
    masks = []
    for k in range(KD):
        first = jnp.int32(0)
        for t in range(slots if k > 0 else 0):
            first = first + jnp.where(owner_ref[t] < k, TILE, 0)
        live = (lane >= first) & (lane < first + length_ref[k])
        masks.append(jnp.where(live, 1.0, 0.0).astype(jnp.bfloat16))
    summed = jnp.concatenate([part_ref[peer] for peer in range(peers)], axis=1)
    for k in range(KD):
        p_ref[k * R : (k + 1) * R, :] = summed * masks[k]
    hmat = h_ref[...]
    wmat = w_ref[...].T
    hgram = lax.dot_general(
        hmat, hmat, (((0,), (0,)), ((), ())), precision=highest, preferred_element_type=jnp.float32
    )
    products = lax.dot_general(summed, p_ref[...], LANES, preferred_element_type=jnp.float32)
    wide_eye = jnp.where(
        lax.broadcasted_iota(jnp.int32, (R, 2 * R), 0) == lax.broadcasted_iota(jnp.int32, (R, 2 * R), 1), 1.5, 0.0
    )
    column_rows = [
        jnp.sum(jnp.where(eye, wmat[:, k : k + 1], 0.0), axis=0, keepdims=True) for k in range(KD)
    ]
    both = []
    for k in range(KD):
        column = wmat[:, k : k + 1]
        mix = hmat * column_rows[k]
        product = products[:, k * R : (k + 1) * R]
        gram = mm_t(mm(mix, product), mix)
        energy = jnp.sum(product * (hgram * column * column_rows[k]), keepdims=True)
        scale = lax.rsqrt(energy + 1e-06)
        both.append(jnp.concatenate([gram * (scale * scale), mix * scale], axis=1))
    for iteration in range(ITERS):
        steps = [wide_eye - 0.5 * pair for pair in both]
        both = [mm_halves(step[:, 0:R], pair) for step, pair in zip(steps, both)]
        if iteration < ITERS - 1:
            next_grams = [mm_halves(pair[:, 0:R], step) for step, pair in zip(steps, both)]
            first_half = lax.broadcasted_iota(jnp.int32, (R, 2 * R), 1) < R
            both = [jnp.where(first_half, gram, pair) for gram, pair in zip(next_grams, both)]
    parts = [three(pair[:, R : 2 * R]) for pair in both]
    turn_rows = jnp.concatenate(
        [jnp.concatenate([parts[k][i] for k in range(KD)], axis=1) for i in range(3)], axis=0
    )
    chunk = 2 * TILE
    for first in range(0, rows, chunk):
        cols = slice(first, first + chunk)
        terms = jnp.dot(turn_rows, p_ref[:, cols], preferred_element_type=jnp.float32)
        polar = (terms[0:R] + (terms[R : 2 * R] + terms[2 * R : 3 * R])).astype(jnp.bfloat16)
        for k in range(KD):
            p_ref[k * R : (k + 1) * R, cols] = polar * masks[k][:, cols]
    projected = jnp.dot(p_ref[...], s_ref[...], preferred_element_type=jnp.float32)
    vmat = v_ref[...]
    head = jnp.zeros((R, R), jnp.float32)
    for k in range(KD):
        block = projected[k * R : (k + 1) * R, :]
        proj_ref[:, k * width : (k + 1) * width] = block
        head = head + mm_halves(block, vmat * wmat[:, k : k + 1], LANES)
    high, middle, low = [term.astype(jnp.float32) for term in three(w_ref[...])]
    send_ref[...] = jnp.concatenate(
        [
            fold(head),
            jnp.concatenate([high, middle], axis=1),
            jnp.concatenate([low, jnp.zeros_like(low)], axis=1),
        ],
        axis=0,
    ).astype(jnp.bfloat16)


def fold(value):
    return jnp.concatenate([value[0 : R // 2], value[R // 2 :]], axis=1)


def unfold(value):
    return jnp.concatenate([value[:, 0:R], value[:, R : 2 * R]], axis=0)


def wide_halves(value):
    return jnp.concatenate([half.astype(jnp.float32) for half in halves(value)], axis=1)


def middle_kernel(in_ref, v_ref, out_ref, w_buf, gram_buf, *, sizes):
    ny, nz, nc, nx = sizes
    head = jnp.zeros((R // 2, 2 * R), jnp.float32)
    for peer in range(nz):
        value = in_ref[peer].astype(jnp.float32)
        head = head + value[0 : R // 2]
        first, last = value[R // 2 : R // 2 + KD], value[R // 2 + KD :]
        w_buf[peer * KD : (peer + 1) * KD, :] = first[:, 0:R] + (first[:, R:] + last[:, 0:R])
    weights = w_buf[...]
    gram_buf[0:R, :] = lax.dot_general(
        weights, weights, (((0,), (0,)), ((), ())), precision=highest, preferred_element_type=jnp.float32
    )
    vmat = v_ref[...]
    gram_buf[R : 2 * R, :] = mm_t(vmat, vmat)
    w_rows, v_rows = R // nx, R // (ny * nc)
    place = lax.axis_index("y") * nc + lax.axis_index("c")
    w_first = pl.multiple_of(lax.axis_index("x") * w_rows, w_rows)
    v_first = pl.multiple_of(R + place * v_rows, v_rows)
    parts = [
        head,
        wide_halves(gram_buf[pl.ds(w_first, w_rows), :]),
        wide_halves(gram_buf[pl.ds(v_first, v_rows), :]),
    ]
    spare = out_ref.shape[1] - R // 2 - w_rows - v_rows
    if spare:
        parts.append(jnp.zeros((spare, 2 * R), jnp.float32))
    value = jnp.concatenate(parts, axis=0).astype(jnp.bfloat16)
    for peer in range(out_ref.shape[0]):
        out_ref[peer] = value


def head_kernel(pack_ref, proj_ref, w_ref, newh_ref, hp_ref, col_ref, side_ref, *, sizes):
    ny, _, nc, nx = sizes
    w_rows, v_rows = R // nx, R // (ny * nc)
    head = jnp.zeros((R // 2, 2 * R), jnp.float32)
    w_parts, v_parts = [0.0] * nx, [0.0] * (ny * nc)
    for peer in range(pack_ref.shape[0]):
        value = pack_ref[peer].astype(jnp.float32)
        place, x = divmod(peer, nx)
        w_last = R // 2 + w_rows
        head = head + value[0 : R // 2]
        w_parts[x] = w_parts[x] + value[R // 2 : w_last]
        v_parts[place] = v_parts[place] + value[w_last : w_last + v_rows]
    head = unfold(head)
    wgram, fgram = [
        jnp.concatenate([part[:, 0:R] + part[:, R:] for part in parts], axis=0) for parts in (w_parts, v_parts)
    ]
    newh_t = eliminate(jnp.concatenate([fgram * wgram, head.T], axis=1))[:, R:]
    newh_ref[...] = newh_t.T
    wmat = w_ref[...].T
    hp = mm_halves(newh_t, proj_ref[...])
    hp_ref[...] = hp
    width = hp.shape[1] // KD
    col = hp[:, 0:width] * wmat[:, 0:1]
    for k in range(1, KD):
        col = col + hp[:, k * width : (k + 1) * width] * wmat[:, k : k + 1]
    for half in range(width // TILE):
        col_ref[half * R : (half + 1) * R, :] = col[:, half * TILE : (half + 1) * TILE].astype(jnp.bfloat16)
    hgram = mm_t(newh_t, newh_t)
    inverse = eliminate(jnp.concatenate([hgram * wgram, jnp.where(eye_mask(), 1.0, 0.0)], axis=1))[:, R:]
    side_ref[...] = jnp.concatenate([hgram, inverse], axis=1)


def column_kernel(col_ref, hp_ref, inverse_ref, newv_ref, out_ref):
    halves = col_ref.shape[0] // R
    col = jnp.concatenate([col_ref[half * R : (half + 1) * R, :] for half in range(halves)], axis=1)
    newv = mm(inverse_ref[:, R : 2 * R], col)
    newv_ref[...] = newv
    width = newv.shape[1]
    lane = lax.broadcasted_iota(jnp.int32, (R, R), 1)
    terms = jnp.zeros((R, R), jnp.float32)
    for k in range(KD):
        sums = jnp.sum(hp_ref[:, k * width : (k + 1) * width] * newv, axis=1, keepdims=True)
        terms = jnp.where(lane == k, sums, terms)
    value = jnp.concatenate([mm_t(newv, newv), terms], axis=1)
    for peer in range(out_ref.shape[0]):
        out_ref[peer] = value


def weight_kernel(in_ref, side_ref, out_ref):
    value = in_ref[0]
    for peer in range(1, in_ref.shape[0]):
        value = value + in_ref[peer]
    solved = eliminate(jnp.concatenate([side_ref[:, 0:R] * value[:, 0:R], value[:, R : 2 * R]], axis=1))
    out_ref[...] = solved[:, R : R + KD].T


def vmem(count):
    return [pl.BlockSpec(memory_space=pltpu.VMEM)] * count


def params(mib=48):
    return pltpu.CompilerParams(vmem_limit_bytes=mib * 1024 * 1024)


def f32(*shape):
    return jax.ShapeDtypeStruct(shape, jnp.float32)


def exchange(value, axes):
    return lax.all_to_all(value, axes, 0, 0, tiled=True)


def share(value, axes, peers):
    return exchange(jnp.broadcast_to(value[None], (peers,) + value.shape), axes)


def body(sizes, series, lengths, tile_owner, factor_h, factor_v, weights_s):
    ny, nz, nc, nx = sizes
    rows, width = series.shape
    slots = tile_owner.shape[0]
    quarter = rows // nx
    w_rows = weights_s.T
    parts = pl.pallas_call(
        partial_kernel,
        in_specs=[pl.BlockSpec(memory_space=pltpu.HBM)] * 2,
        out_specs=pl.BlockSpec(memory_space=pltpu.VMEM),
        out_shape=jax.ShapeDtypeStruct((nx, R, quarter), jnp.bfloat16),
        scratch_shapes=[
            pltpu.VMEM((R, width), jnp.float32),
            pltpu.VMEM((rows, width), jnp.bfloat16),
            pltpu.SemaphoreType.DMA((nx + 1,)),
        ],
        compiler_params=params(63),
    )(factor_v, series)
    parts = jnp.sum(exchange(parts, "x").astype(jnp.float32), axis=0).astype(jnp.bfloat16)
    parts = share(parts, "x", nx)
    proj, send = pl.pallas_call(
        functools.partial(polar_kernel, peers=nx),
        in_specs=[pl.BlockSpec(memory_space=pltpu.SMEM)] * 2 + vmem(5),
        out_specs=vmem(2),
        out_shape=[f32(R, KD * width), jax.ShapeDtypeStruct((R // 2 + 2 * KD, 2 * R), jnp.bfloat16)],
        scratch_shapes=[
            pltpu.VMEM((KD * R, rows), jnp.bfloat16),
        ],
        compiler_params=params(),
    )(tile_owner, lengths, parts, series, factor_h, factor_v, w_rows)
    near = ny * nc * nx
    share_rows = -(-(R // 2 + R // nx + R // (ny * nc)) // 16) * 16
    pieces = pl.pallas_call(
        functools.partial(middle_kernel, sizes=sizes),
        in_specs=vmem(2),
        out_specs=pl.BlockSpec(memory_space=pltpu.VMEM),
        out_shape=jax.ShapeDtypeStruct((near, share_rows, 2 * R), jnp.bfloat16),
        scratch_shapes=[pltpu.VMEM((nz * KD, R), jnp.float32), pltpu.VMEM((2 * R, R), jnp.float32)],
        compiler_params=params(),
    )(share(send, "z", nz), factor_v)
    pieces = exchange(pieces, ("y", "c", "x"))
    new_h, hp, col, side = pl.pallas_call(
        functools.partial(head_kernel, sizes=sizes),
        in_specs=vmem(3),
        out_specs=vmem(4),
        out_shape=[f32(R, R), f32(R, KD * width), jax.ShapeDtypeStruct((R * width // TILE, TILE), jnp.bfloat16), f32(R, 2 * R)],
        compiler_params=params(),
    )(pieces, proj, w_rows)
    near = ny * nc
    pieces = exchange(col.reshape(near, col.shape[0] // near, TILE), ("y", "c"))
    pieces = share(jnp.sum(pieces.astype(jnp.float32), axis=0).astype(jnp.bfloat16), "z", nz).astype(jnp.float32)
    pieces = share(jnp.sum(pieces, axis=0), ("y", "c"), near)
    new_v, sums = pl.pallas_call(
        column_kernel,
        in_specs=vmem(3),
        out_specs=vmem(2),
        out_shape=[f32(R, width), f32(nx, R, 2 * R)],
        compiler_params=params(),
    )(pieces.reshape(col.shape), hp, side)
    new_s = pl.pallas_call(
        weight_kernel,
        in_specs=vmem(2),
        out_specs=pl.BlockSpec(memory_space=pltpu.VMEM),
        out_shape=f32(KD, R),
        compiler_params=params(),
    )(exchange(sums, "x"), side)
    return (new_h, new_v, new_s.T)


def solution(mesh):
    traj, nx = mesh.devices.shape
    ny, nc = (4, 2) if traj % 128 == 0 else (2, 2)
    sizes = (ny, traj // (ny * nc), nc, nx)
    fine = Mesh(mesh.devices.reshape(sizes), ("y", "z", "c", "x"))
    traj_axes = ("y", "z", "c")
    return jax.shard_map(
        functools.partial(body, sizes),
        mesh=fine,
        in_specs=(P(traj_axes, "x"), P(traj_axes), P(traj_axes), P(), P(None, "x"), P(None, traj_axes)),
        out_specs=(P(), P(None, "x"), P(None, traj_axes)),
        check_vma=False,
    )
```

```python
import functools

import jax
import jax.numpy as jnp
from jax import lax
from jax.experimental import pallas as pl
from jax.experimental.pallas import tpu as pltpu
from jax.sharding import Mesh, PartitionSpec as P

ITERS = 8
R = 64
TILE = 128
KD = 4
LANES = (((1,), (1,)), ((), ()))

highest = lax.Precision.HIGHEST


def mm(left, right):
    return jnp.dot(left, right, precision=highest, preferred_element_type=jnp.float32)


def mm_t(left, right):
    return lax.dot_general(left, right, LANES, precision=highest, preferred_element_type=jnp.float32)


def halves(value):
    high = value.astype(jnp.bfloat16)
    return high, (value - high.astype(jnp.float32)).astype(jnp.bfloat16)


def mm_halves(left, right, dims=(((1,), (0,)), ((), ()))):
    rows, cols = left.shape[0], right.shape[1 - dims[0][1][0]]
    left = jnp.concatenate(halves(left), axis=0)
    right = jnp.concatenate(halves(right), axis=1 - dims[0][1][0])
    terms = lax.dot_general(left, right, dims, preferred_element_type=jnp.float32)
    return terms[0:rows, 0:cols] + (terms[0:rows, cols:] + terms[rows:, 0:cols])


def eye_mask():
    rows = lax.broadcasted_iota(jnp.int32, (R, R), 0)
    cols = lax.broadcasted_iota(jnp.int32, (R, R), 1)
    return rows == cols


def eliminate(both, block=8):
    rows = lax.broadcasted_iota(jnp.int32, both.shape, 0)
    for k in range(0, R, block):
        col = [jnp.broadcast_to(both[:, k + i : k + i + 1], both.shape) for i in range(block)]
        row = [both[k + i : k + i + 1, :] for i in range(block)]
        piv = [[col[j][k + i : k + i + 1, :] for j in range(block)] for i in range(block)]
        for q in range(0, block, 2):
            inv = 1.0 / (piv[q][q] * piv[q + 1][q + 1] - piv[q][q + 1] * piv[q + 1][q])
            a00, a01 = piv[q + 1][q + 1] * inv, -piv[q][q + 1] * inv
            a10, a11 = -piv[q + 1][q] * inv, piv[q][q] * inv
            new0, new1 = a00 * row[q] + a01 * row[q + 1], a10 * row[q] + a11 * row[q + 1]
            later = range(q + 2, block)
            solved = {
                j: (a00 * piv[q][j] + a01 * piv[q + 1][j], a10 * piv[q][j] + a11 * piv[q + 1][j])
                for j in later
            }
            for i in range(block):
                if i in (q, q + 1):
                    continue
                row[i] = row[i] - (piv[i][q] * new0 + piv[i][q + 1] * new1)
                for j in later:
                    piv[i][j] = piv[i][j] - (piv[i][q] * solved[j][0] + piv[i][q + 1] * solved[j][1])
            row[q], row[q + 1] = new0, new1
            for j in later:
                piv[q][j], piv[q + 1][j] = solved[j]
        rest = both
        for i in range(0, block, 2):
            rest = rest - (col[i] * row[i] + col[i + 1] * row[i + 1])
        for i in range(block):
            rest = jnp.where(rows == k + i, row[i], rest)
        both = rest
    return both


def partial_kernel(v_ref, s_ref, out_ref, v_buf, s_buf, sems):
    count, _, quarter = out_ref.shape
    pieces = 2
    step = count * quarter // pieces
    copies = [pltpu.make_async_copy(v_ref, v_buf, sems.at[pieces])]
    for i in range(pieces):
        rows = pl.ds(i * step, step)
        copies.append(pltpu.make_async_copy(s_ref.at[rows, :], s_buf.at[rows, :], sems.at[i]))
    for copy in copies:
        copy.start()
    copies[0].wait()
    factor_bf = v_buf[...].astype(jnp.bfloat16)
    for i in range(pieces):
        copies[i + 1].wait()
        for peer in range(i * count // pieces, max((i + 1) * count // pieces, i * count // pieces + 1)):
            out_ref[peer] = lax.dot_general(
                factor_bf, s_buf[peer * quarter : (peer + 1) * quarter, :], LANES, preferred_element_type=jnp.float32
            ).astype(jnp.bfloat16)


def three(value):
    high = value.astype(jnp.bfloat16)
    rest = value - high.astype(jnp.float32)
    middle = rest.astype(jnp.bfloat16)
    return high, middle, (rest - middle.astype(jnp.float32)).astype(jnp.bfloat16)


def polar_kernel(
    owner_ref, length_ref, part_ref, s_ref, h_ref, w_ref, proj_ref, send_ref, p_ref, head_buf, *, peers
):
    rows, width = s_ref.shape
    slots = rows // TILE
    eye = eye_mask()
    lane = lax.broadcasted_iota(jnp.int32, (1, rows), 1)
    masks = []
    for k in range(KD):
        first = jnp.int32(0)
        for t in range(slots if k > 0 else 0):
            first = first + jnp.where(owner_ref[t] < k, TILE, 0)
        live = (lane >= first) & (lane < first + length_ref[k])
        masks.append(jnp.where(live, 1.0, 0.0).astype(jnp.bfloat16))
    summed = jnp.concatenate([part_ref[peer] for peer in range(peers)], axis=1)
    for k in range(KD):
        p_ref[k * R : (k + 1) * R, :] = summed * masks[k]
    hmat = h_ref[...]
    wmat = w_ref[...].T
    hgram = lax.dot_general(
        hmat, hmat, (((0,), (0,)), ((), ())), precision=highest, preferred_element_type=jnp.float32
    )
    products = lax.dot_general(summed, p_ref[...], LANES, preferred_element_type=jnp.float32)
    wide_eye = jnp.where(
        lax.broadcasted_iota(jnp.int32, (R, 2 * R), 0) == lax.broadcasted_iota(jnp.int32, (R, 2 * R), 1), 1.5, 0.0
    )
    column_rows = [
        jnp.sum(jnp.where(eye, wmat[:, k : k + 1], 0.0), axis=0, keepdims=True) for k in range(KD)
    ]
    both = []
    for k in range(KD):
        column = wmat[:, k : k + 1]
        mix = hmat * column_rows[k]
        product = products[:, k * R : (k + 1) * R]
        gram = mm_t(mm(mix, product), mix)
        energy = jnp.sum(product * (hgram * column * column_rows[k]), keepdims=True)
        scale = lax.rsqrt(energy + 1e-06)
        both.append(jnp.concatenate([gram * (scale * scale), mix * scale], axis=1))
    for iteration in range(ITERS):
        steps = [wide_eye - 0.5 * pair for pair in both]
        both = [mm_halves(step[:, 0:R], pair) for step, pair in zip(steps, both)]
        if iteration < ITERS - 1:
            next_grams = [mm_halves(pair[:, 0:R], step) for step, pair in zip(steps, both)]
            first_half = lax.broadcasted_iota(jnp.int32, (R, 2 * R), 1) < R
            both = [jnp.where(first_half, gram, pair) for gram, pair in zip(next_grams, both)]
    parts = [three(pair[:, R : 2 * R]) for pair in both]
    turn_rows = jnp.concatenate(
        [jnp.concatenate([parts[k][i] for k in range(KD)], axis=1) for i in range(3)], axis=0
    )
    chunk = 2 * TILE
    for first in range(0, rows, chunk):
        cols = slice(first, first + chunk)
        terms = jnp.dot(turn_rows, p_ref[:, cols], preferred_element_type=jnp.float32)
        polar = (terms[0:R] + (terms[R : 2 * R] + terms[2 * R : 3 * R])).astype(jnp.bfloat16)
        for k in range(KD):
            p_ref[k * R : (k + 1) * R, cols] = polar * masks[k][:, cols]
    projected = jnp.dot(p_ref[...], s_ref[...], preferred_element_type=jnp.float32)
    heads = lax.dot_general(p_ref[...], summed, LANES, preferred_element_type=jnp.float32)
    head = jnp.zeros((R, R), jnp.float32)
    for k in range(KD):
        proj_ref[:, k * width : (k + 1) * width] = projected[k * R : (k + 1) * R, :]
        head = head + heads[k * R : (k + 1) * R, :] * column_rows[k]
    head_buf[...] = head
    share_rows = R // peers
    first = pl.multiple_of(lax.axis_index("x") * share_rows, share_rows)
    high, middle, low = [term.astype(jnp.float32) for term in three(w_ref[...])]
    send_ref[...] = jnp.concatenate(
        [
            fold(head_buf[pl.ds(first, share_rows), :]),
            jnp.concatenate([high, middle], axis=1),
            jnp.concatenate([low, jnp.zeros_like(low)], axis=1),
        ],
        axis=0,
    ).astype(jnp.bfloat16)


def fold(value):
    half = value.shape[0] // 2
    return jnp.concatenate([value[0:half], value[half:]], axis=1)


def unfold(value):
    return jnp.concatenate([value[:, 0:R], value[:, R : 2 * R]], axis=0)


def wide_halves(value):
    return jnp.concatenate([half.astype(jnp.float32) for half in halves(value)], axis=1)


def middle_kernel(in_ref, v_ref, out_ref, w_buf, gram_buf, *, sizes):
    ny, nz, nc, nx = sizes
    h_rows = R // nx // 2
    head = jnp.zeros((h_rows, 2 * R), jnp.float32)
    for peer in range(nz):
        value = in_ref[peer].astype(jnp.float32)
        head = head + value[0:h_rows]
        first, last = value[h_rows : h_rows + KD], value[h_rows + KD :]
        w_buf[peer * KD : (peer + 1) * KD, :] = first[:, 0:R] + (first[:, R:] + last[:, 0:R])
    weights = w_buf[...]
    gram_buf[0:R, :] = lax.dot_general(
        weights, weights, (((0,), (0,)), ((), ())), precision=highest, preferred_element_type=jnp.float32
    )
    vmat = v_ref[...]
    gram_buf[R : 2 * R, :] = mm_t(vmat, vmat)
    w_rows, v_rows = R // nx, R // (ny * nc)
    place = lax.axis_index("y") * nc + lax.axis_index("c")
    w_first = pl.multiple_of(lax.axis_index("x") * w_rows, w_rows)
    v_first = pl.multiple_of(R + place * v_rows, v_rows)
    parts = [
        head,
        wide_halves(gram_buf[pl.ds(w_first, w_rows), :]),
        wide_halves(gram_buf[pl.ds(v_first, v_rows), :]),
    ]
    value = jnp.concatenate(parts, axis=0).astype(jnp.bfloat16)
    for peer in range(out_ref.shape[0]):
        out_ref[peer] = value


def head_kernel(pack_ref, proj_ref, w_ref, newh_ref, hp_ref, col_ref, side_ref, *, sizes):
    ny, _, nc, nx = sizes
    h_rows, w_rows, v_rows = R // nx // 2, R // nx, R // (ny * nc)
    w_last = h_rows + w_rows
    h_parts, w_parts, v_parts = [0.0] * nx, [0.0] * nx, [0.0] * (ny * nc)
    for peer in range(pack_ref.shape[0]):
        value = pack_ref[peer].astype(jnp.float32)
        place, x = divmod(peer, nx)
        h_parts[x] = h_parts[x] + value[0:h_rows]
        w_parts[x] = w_parts[x] + value[h_rows:w_last]
        v_parts[place] = v_parts[place] + value[w_last : w_last + v_rows]
    head = jnp.concatenate([unfold(part) for part in h_parts], axis=0)
    wgram, fgram = [
        jnp.concatenate([part[:, 0:R] + part[:, R:] for part in parts], axis=0) for parts in (w_parts, v_parts)
    ]
    newh_t = eliminate(jnp.concatenate([fgram * wgram, head.T], axis=1))[:, R:]
    newh_ref[...] = newh_t.T
    wmat = w_ref[...].T
    hp = mm_halves(newh_t, proj_ref[...])
    hp_ref[...] = hp
    width = hp.shape[1] // KD
    col = hp[:, 0:width] * wmat[:, 0:1]
    for k in range(1, KD):
        col = col + hp[:, k * width : (k + 1) * width] * wmat[:, k : k + 1]
    for half in range(width // TILE):
        col_ref[half * R : (half + 1) * R, :] = col[:, half * TILE : (half + 1) * TILE].astype(jnp.bfloat16)
    hgram = mm_t(newh_t, newh_t)
    inverse = eliminate(jnp.concatenate([hgram * wgram, jnp.where(eye_mask(), 1.0, 0.0)], axis=1))[:, R:]
    side_ref[...] = jnp.concatenate([hgram, inverse], axis=1)


def column_kernel(col_ref, hp_ref, inverse_ref, newv_ref, out_ref):
    halves = col_ref.shape[0] // R
    col = jnp.concatenate([col_ref[half * R : (half + 1) * R, :] for half in range(halves)], axis=1)
    newv = mm(inverse_ref[:, R : 2 * R], col)
    newv_ref[...] = newv
    width = newv.shape[1]
    lane = lax.broadcasted_iota(jnp.int32, (R, R), 1)
    terms = jnp.zeros((R, R), jnp.float32)
    for k in range(KD):
        sums = jnp.sum(hp_ref[:, k * width : (k + 1) * width] * newv, axis=1, keepdims=True)
        terms = jnp.where(lane == k, sums, terms)
    value = jnp.concatenate([mm_t(newv, newv), terms], axis=1)
    for peer in range(out_ref.shape[0]):
        out_ref[peer] = value


def weight_kernel(in_ref, side_ref, out_ref):
    value = in_ref[0]
    for peer in range(1, in_ref.shape[0]):
        value = value + in_ref[peer]
    solved = eliminate(jnp.concatenate([side_ref[:, 0:R] * value[:, 0:R], value[:, R : 2 * R]], axis=1))
    out_ref[...] = solved[:, R : R + KD].T


def vmem(count):
    return [pl.BlockSpec(memory_space=pltpu.VMEM)] * count


def params(mib=48):
    return pltpu.CompilerParams(vmem_limit_bytes=mib * 1024 * 1024)


def f32(*shape):
    return jax.ShapeDtypeStruct(shape, jnp.float32)


def exchange(value, axes):
    return lax.all_to_all(value, axes, 0, 0, tiled=True)


def share(value, axes, peers):
    return exchange(jnp.broadcast_to(value[None], (peers,) + value.shape), axes)


def body(sizes, series, lengths, tile_owner, factor_h, factor_v, weights_s):
    ny, nz, nc, nx = sizes
    rows, width = series.shape
    slots = tile_owner.shape[0]
    quarter = rows // nx
    w_rows = weights_s.T
    parts = pl.pallas_call(
        partial_kernel,
        in_specs=[pl.BlockSpec(memory_space=pltpu.HBM)] * 2,
        out_specs=pl.BlockSpec(memory_space=pltpu.VMEM),
        out_shape=jax.ShapeDtypeStruct((nx, R, quarter), jnp.bfloat16),
        scratch_shapes=[
            pltpu.VMEM((R, width), jnp.float32),
            pltpu.VMEM((rows, width), jnp.bfloat16),
            pltpu.SemaphoreType.DMA((nx + 1,)),
        ],
        compiler_params=params(63),
    )(factor_v, series)
    parts = jnp.sum(exchange(parts, "x").astype(jnp.float32), axis=0).astype(jnp.bfloat16)
    parts = share(parts, "x", nx)
    proj, send = pl.pallas_call(
        functools.partial(polar_kernel, peers=nx),
        in_specs=[pl.BlockSpec(memory_space=pltpu.SMEM)] * 2 + vmem(4),
        out_specs=vmem(2),
        out_shape=[f32(R, KD * width), jax.ShapeDtypeStruct((R // nx // 2 + 2 * KD, 2 * R), jnp.bfloat16)],
        scratch_shapes=[
            pltpu.VMEM((KD * R, rows), jnp.bfloat16),
            pltpu.VMEM((R, R), jnp.float32),
        ],
        compiler_params=params(),
    )(tile_owner, lengths, parts, series, factor_h, w_rows)
    near = ny * nc * nx
    share_rows = R // nx // 2 + R // nx + R // (ny * nc)
    pieces = pl.pallas_call(
        functools.partial(middle_kernel, sizes=sizes),
        in_specs=vmem(2),
        out_specs=pl.BlockSpec(memory_space=pltpu.VMEM),
        out_shape=jax.ShapeDtypeStruct((near, share_rows, 2 * R), jnp.bfloat16),
        scratch_shapes=[pltpu.VMEM((nz * KD, R), jnp.float32), pltpu.VMEM((2 * R, R), jnp.float32)],
        compiler_params=params(),
    )(share(send, "z", nz), factor_v)
    pieces = exchange(pieces, ("y", "c", "x"))
    new_h, hp, col, side = pl.pallas_call(
        functools.partial(head_kernel, sizes=sizes),
        in_specs=vmem(3),
        out_specs=vmem(4),
        out_shape=[f32(R, R), f32(R, KD * width), jax.ShapeDtypeStruct((R * width // TILE, TILE), jnp.bfloat16), f32(R, 2 * R)],
        compiler_params=params(),
    )(pieces, proj, w_rows)
    near = ny * nc
    pieces = exchange(col.reshape(near, col.shape[0] // near, TILE), ("y", "c"))
    pieces = share(jnp.sum(pieces.astype(jnp.float32), axis=0).astype(jnp.bfloat16), "z", nz).astype(jnp.float32)
    pieces = share(jnp.sum(pieces, axis=0), ("y", "c"), near)
    new_v, sums = pl.pallas_call(
        column_kernel,
        in_specs=vmem(3),
        out_specs=vmem(2),
        out_shape=[f32(R, width), f32(nx, R, 2 * R)],
        compiler_params=params(),
    )(pieces.reshape(col.shape), hp, side)
    new_s = pl.pallas_call(
        weight_kernel,
        in_specs=vmem(2),
        out_specs=pl.BlockSpec(memory_space=pltpu.VMEM),
        out_shape=f32(KD, R),
        compiler_params=params(),
    )(exchange(sums, "x"), side)
    return (new_h, new_v, new_s.T)


def solution(mesh):
    traj, nx = mesh.devices.shape
    ny, nc = (4, 2) if traj % 128 == 0 else (2, 2)
    sizes = (ny, traj // (ny * nc), nc, nx)
    fine = Mesh(mesh.devices.reshape(sizes), ("y", "z", "c", "x"))
    traj_axes = ("y", "z", "c")
    return jax.shard_map(
        functools.partial(body, sizes),
        mesh=fine,
        in_specs=(P(traj_axes, "x"), P(traj_axes), P(traj_axes), P(), P(None, "x"), P(None, traj_axes)),
        out_specs=(P(), P(None, "x"), P(None, traj_axes)),
        check_vma=False,
    )
```

```python
import functools

import jax
import jax.numpy as jnp
from jax import lax
from jax.experimental import pallas as pl
from jax.experimental.pallas import tpu as pltpu
from jax.sharding import Mesh, PartitionSpec as P

ITERS = 8
R = 64
TILE = 128
KD = 4
LANES = (((1,), (1,)), ((), ()))

highest = lax.Precision.HIGHEST


def mm(left, right):
    return jnp.dot(left, right, precision=highest, preferred_element_type=jnp.float32)


def mm_t(left, right):
    return lax.dot_general(left, right, LANES, precision=highest, preferred_element_type=jnp.float32)


def halves(value):
    high = value.astype(jnp.bfloat16)
    return high, (value - high.astype(jnp.float32)).astype(jnp.bfloat16)


def mm_halves(left, right, dims=(((1,), (0,)), ((), ()))):
    rows, cols = left.shape[0], right.shape[1 - dims[0][1][0]]
    left = jnp.concatenate(halves(left), axis=0)
    right = jnp.concatenate(halves(right), axis=1 - dims[0][1][0])
    terms = lax.dot_general(left, right, dims, preferred_element_type=jnp.float32)
    return terms[0:rows, 0:cols] + (terms[0:rows, cols:] + terms[rows:, 0:cols])


def eye_mask():
    rows = lax.broadcasted_iota(jnp.int32, (R, R), 0)
    cols = lax.broadcasted_iota(jnp.int32, (R, R), 1)
    return rows == cols


def eliminate(both, block=8):
    rows = lax.broadcasted_iota(jnp.int32, both.shape, 0)
    for k in range(0, R, block):
        col = [jnp.broadcast_to(both[:, k + i : k + i + 1], both.shape) for i in range(block)]
        row = [both[k + i : k + i + 1, :] for i in range(block)]
        piv = [[col[j][k + i : k + i + 1, :] for j in range(block)] for i in range(block)]
        for q in range(0, block, 2):
            inv = 1.0 / (piv[q][q] * piv[q + 1][q + 1] - piv[q][q + 1] * piv[q + 1][q])
            a00, a01 = piv[q + 1][q + 1] * inv, -piv[q][q + 1] * inv
            a10, a11 = -piv[q + 1][q] * inv, piv[q][q] * inv
            new0, new1 = a00 * row[q] + a01 * row[q + 1], a10 * row[q] + a11 * row[q + 1]
            later = range(q + 2, block)
            solved = {
                j: (a00 * piv[q][j] + a01 * piv[q + 1][j], a10 * piv[q][j] + a11 * piv[q + 1][j])
                for j in later
            }
            for i in range(block):
                if i in (q, q + 1):
                    continue
                row[i] = row[i] - (piv[i][q] * new0 + piv[i][q + 1] * new1)
                for j in later:
                    piv[i][j] = piv[i][j] - (piv[i][q] * solved[j][0] + piv[i][q + 1] * solved[j][1])
            row[q], row[q + 1] = new0, new1
            for j in later:
                piv[q][j], piv[q + 1][j] = solved[j]
        rest = both
        for i in range(0, block, 2):
            rest = rest - (col[i] * row[i] + col[i + 1] * row[i + 1])
        for i in range(block):
            rest = jnp.where(rows == k + i, row[i], rest)
        both = rest
    return both


def partial_kernel(v_ref, s_ref, out_ref, planes_ref, v_buf, s_buf, sems):
    count, _, quarter = out_ref.shape
    pieces = 2
    step = count * quarter // pieces
    copies = [pltpu.make_async_copy(v_ref, v_buf, sems.at[pieces])]
    for i in range(pieces):
        rows = pl.ds(i * step, step)
        copies.append(pltpu.make_async_copy(s_ref.at[rows, :], s_buf.at[rows, :], sems.at[i]))
    for copy in copies:
        copy.start()
    copies[0].wait()
    vmat = v_buf[...]
    factor_bf = vmat.astype(jnp.bfloat16)
    planes_ref[...] = wide_halves(mm_t(vmat, vmat)).astype(jnp.bfloat16)
    for i in range(pieces):
        copies[i + 1].wait()
        for peer in range(i * count // pieces, max((i + 1) * count // pieces, i * count // pieces + 1)):
            out_ref[peer] = lax.dot_general(
                factor_bf, s_buf[peer * quarter : (peer + 1) * quarter, :], LANES, preferred_element_type=jnp.float32
            ).astype(jnp.bfloat16)


def three(value):
    high = value.astype(jnp.bfloat16)
    rest = value - high.astype(jnp.float32)
    middle = rest.astype(jnp.bfloat16)
    return high, middle, (rest - middle.astype(jnp.float32)).astype(jnp.bfloat16)


def polar_kernel(
    owner_ref, length_ref, part_ref, s_ref, h_ref, w_ref, proj_ref, send_ref, fgram_ref, p_ref, *, peers
):
    rows, width = s_ref.shape
    slots = rows // TILE
    eye = eye_mask()
    lane = lax.broadcasted_iota(jnp.int32, (1, rows), 1)
    masks = []
    for k in range(KD):
        first = jnp.int32(0)
        for t in range(slots if k > 0 else 0):
            first = first + jnp.where(owner_ref[t] < k, TILE, 0)
        live = (lane >= first) & (lane < first + length_ref[k])
        masks.append(jnp.where(live, 1.0, 0.0).astype(jnp.bfloat16))
    base = rows // peers
    summed = jnp.concatenate([part_ref[peer, :, 0:base] for peer in range(peers)], axis=1)
    planes = part_ref[0, :, base:].astype(jnp.float32)
    for peer in range(1, peers):
        planes = planes + part_ref[peer, :, base:].astype(jnp.float32)
    fgram_ref[...] = planes[:, 0:R] + planes[:, R:]
    for k in range(KD):
        p_ref[k * R : (k + 1) * R, :] = summed * masks[k]
    hmat = h_ref[...]
    wmat = w_ref[...].T
    hgram = lax.dot_general(
        hmat, hmat, (((0,), (0,)), ((), ())), precision=highest, preferred_element_type=jnp.float32
    )
    products = lax.dot_general(summed, p_ref[...], LANES, preferred_element_type=jnp.float32)
    wide_eye = jnp.where(
        lax.broadcasted_iota(jnp.int32, (R, 2 * R), 0) == lax.broadcasted_iota(jnp.int32, (R, 2 * R), 1), 1.5, 0.0
    )
    column_rows = [
        jnp.sum(jnp.where(eye, wmat[:, k : k + 1], 0.0), axis=0, keepdims=True) for k in range(KD)
    ]
    both = []
    for k in range(KD):
        column = wmat[:, k : k + 1]
        mix = hmat * column_rows[k]
        product = products[:, k * R : (k + 1) * R]
        gram = mm_t(mm(mix, product), mix)
        energy = jnp.sum(product * (hgram * column * column_rows[k]), keepdims=True)
        scale = lax.rsqrt(energy + 1e-06)
        both.append(jnp.concatenate([gram * (scale * scale), mix * scale], axis=1))
    for iteration in range(ITERS):
        steps = [wide_eye - 0.5 * pair for pair in both]
        both = [mm_halves(step[:, 0:R], pair) for step, pair in zip(steps, both)]
        if iteration < ITERS - 1:
            next_grams = [mm_halves(pair[:, 0:R], step) for step, pair in zip(steps, both)]
            first_half = lax.broadcasted_iota(jnp.int32, (R, 2 * R), 1) < R
            both = [jnp.where(first_half, gram, pair) for gram, pair in zip(next_grams, both)]
    parts = [three(pair[:, R : 2 * R]) for pair in both]
    turn_rows = jnp.concatenate(
        [jnp.concatenate([parts[k][i] for k in range(KD)], axis=1) for i in range(3)], axis=0
    )
    chunk = 2 * TILE
    for first in range(0, rows, chunk):
        cols = slice(first, first + chunk)
        terms = jnp.dot(turn_rows, p_ref[:, cols], preferred_element_type=jnp.float32)
        polar = (terms[0:R] + (terms[R : 2 * R] + terms[2 * R : 3 * R])).astype(jnp.bfloat16)
        for k in range(KD):
            p_ref[k * R : (k + 1) * R, cols] = polar * masks[k][:, cols]
    projected = jnp.dot(p_ref[...], s_ref[...], preferred_element_type=jnp.float32)
    heads = lax.dot_general(p_ref[...], summed, LANES, preferred_element_type=jnp.float32)
    head = jnp.zeros((R, R), jnp.float32)
    for k in range(KD):
        proj_ref[:, k * width : (k + 1) * width] = projected[k * R : (k + 1) * R, :]
        head = head + heads[k * R : (k + 1) * R, :] * column_rows[k]
    high, middle, low = [term.astype(jnp.float32) for term in three(w_ref[...])]
    send_ref[...] = jnp.concatenate(
        [
            fold(head),
            jnp.concatenate([high, middle], axis=1),
            jnp.concatenate([low, jnp.zeros_like(low)], axis=1),
        ],
        axis=0,
    ).astype(jnp.bfloat16)


def fold(value):
    half = value.shape[0] // 2
    return jnp.concatenate([value[0:half], value[half:]], axis=1)


def unfold(value):
    return jnp.concatenate([value[:, 0:R], value[:, R : 2 * R]], axis=0)


def wide_halves(value):
    return jnp.concatenate([half.astype(jnp.float32) for half in halves(value)], axis=1)


def middle_kernel(in_ref, out_ref, w_buf):
    half = R // 2
    head = jnp.zeros((half, 2 * R), jnp.float32)
    for peer in range(in_ref.shape[0]):
        value = in_ref[peer].astype(jnp.float32)
        head = head + value[0:half]
        first, last = value[half : half + KD], value[half + KD :]
        w_buf[peer * KD : (peer + 1) * KD, :] = first[:, 0:R] + (first[:, R:] + last[:, 0:R])
    weights = w_buf[...]
    wgram = lax.dot_general(
        weights, weights, (((0,), (0,)), ((), ())), precision=highest, preferred_element_type=jnp.float32
    )
    value = jnp.concatenate([head, wide_halves(wgram)], axis=0).astype(jnp.bfloat16)
    for peer in range(out_ref.shape[0]):
        out_ref[peer] = value


def head_kernel(pack_ref, fgram_ref, proj_ref, w_ref, newh_ref, hp_ref, col_ref, side_ref):
    value = pack_ref[0].astype(jnp.float32)
    for peer in range(1, pack_ref.shape[0]):
        value = value + pack_ref[peer].astype(jnp.float32)
    head = unfold(value[0 : R // 2])
    wgram = value[R // 2 :, 0:R] + value[R // 2 :, R:]
    fgram = fgram_ref[...]
    newh_t = eliminate(jnp.concatenate([fgram * wgram, head.T], axis=1))[:, R:]
    newh_ref[...] = newh_t.T
    wmat = w_ref[...].T
    hp = mm_halves(newh_t, proj_ref[...])
    hp_ref[...] = hp
    width = hp.shape[1] // KD
    col = hp[:, 0:width] * wmat[:, 0:1]
    for k in range(1, KD):
        col = col + hp[:, k * width : (k + 1) * width] * wmat[:, k : k + 1]
    for half in range(width // TILE):
        col_ref[half * R : (half + 1) * R, :] = col[:, half * TILE : (half + 1) * TILE].astype(jnp.bfloat16)
    hgram = mm_t(newh_t, newh_t)
    inverse = eliminate(jnp.concatenate([hgram * wgram, jnp.where(eye_mask(), 1.0, 0.0)], axis=1))[:, R:]
    side_ref[...] = jnp.concatenate([hgram, inverse], axis=1)


def column_kernel(col_ref, hp_ref, inverse_ref, newv_ref, out_ref):
    halves = col_ref.shape[0] // R
    col = jnp.concatenate([col_ref[half * R : (half + 1) * R, :] for half in range(halves)], axis=1)
    newv = mm(inverse_ref[:, R : 2 * R], col)
    newv_ref[...] = newv
    width = newv.shape[1]
    lane = lax.broadcasted_iota(jnp.int32, (R, R), 1)
    terms = jnp.zeros((R, R), jnp.float32)
    for k in range(KD):
        sums = jnp.sum(hp_ref[:, k * width : (k + 1) * width] * newv, axis=1, keepdims=True)
        terms = jnp.where(lane == k, sums, terms)
    value = jnp.concatenate([mm_t(newv, newv), terms], axis=1)
    for peer in range(out_ref.shape[0]):
        out_ref[peer] = value


def weight_kernel(in_ref, side_ref, out_ref):
    value = in_ref[0]
    for peer in range(1, in_ref.shape[0]):
        value = value + in_ref[peer]
    solved = eliminate(jnp.concatenate([side_ref[:, 0:R] * value[:, 0:R], value[:, R : 2 * R]], axis=1))
    out_ref[...] = solved[:, R : R + KD].T


def vmem(count):
    return [pl.BlockSpec(memory_space=pltpu.VMEM)] * count


def params(mib=48):
    return pltpu.CompilerParams(vmem_limit_bytes=mib * 1024 * 1024)


def f32(*shape):
    return jax.ShapeDtypeStruct(shape, jnp.float32)


def exchange(value, axes):
    return lax.all_to_all(value, axes, 0, 0, tiled=True)


def share(value, axes, peers):
    return exchange(jnp.broadcast_to(value[None], (peers,) + value.shape), axes)


def body(sizes, series, lengths, tile_owner, factor_h, factor_v, weights_s):
    ny, nz, nc, nx = sizes
    rows, width = series.shape
    slots = tile_owner.shape[0]
    quarter = rows // nx
    w_rows = weights_s.T
    parts, planes = pl.pallas_call(
        partial_kernel,
        in_specs=[pl.BlockSpec(memory_space=pltpu.HBM)] * 2,
        out_specs=vmem(2),
        out_shape=[
            jax.ShapeDtypeStruct((nx, R, quarter), jnp.bfloat16),
            jax.ShapeDtypeStruct((R, 2 * R), jnp.bfloat16),
        ],
        scratch_shapes=[
            pltpu.VMEM((R, width), jnp.float32),
            pltpu.VMEM((rows, width), jnp.bfloat16),
            pltpu.SemaphoreType.DMA((nx + 1,)),
        ],
        compiler_params=params(63),
    )(factor_v, series)
    parts = jnp.sum(exchange(parts, "x").astype(jnp.float32), axis=0).astype(jnp.bfloat16)
    parts = share(jnp.concatenate([parts, planes], axis=1), "x", nx)
    proj, send, fgram = pl.pallas_call(
        functools.partial(polar_kernel, peers=nx),
        in_specs=[pl.BlockSpec(memory_space=pltpu.SMEM)] * 2 + vmem(4),
        out_specs=vmem(3),
        out_shape=[
            f32(R, KD * width),
            jax.ShapeDtypeStruct((R // 2 + 2 * KD, 2 * R), jnp.bfloat16),
            f32(R, R),
        ],
        scratch_shapes=[
            pltpu.VMEM((KD * R, rows), jnp.bfloat16),
        ],
        compiler_params=params(),
    )(tile_owner, lengths, parts, series, factor_h, w_rows)
    near = ny * nc
    pieces = pl.pallas_call(
        middle_kernel,
        in_specs=vmem(1),
        out_specs=pl.BlockSpec(memory_space=pltpu.VMEM),
        out_shape=jax.ShapeDtypeStruct((near, R // 2 + R, 2 * R), jnp.bfloat16),
        scratch_shapes=[pltpu.VMEM((nz * KD, R), jnp.float32)],
        compiler_params=params(),
    )(share(send, "z", nz))
    pieces = exchange(pieces, ("y", "c"))
    new_h, hp, col, side = pl.pallas_call(
        head_kernel,
        in_specs=vmem(4),
        out_specs=vmem(4),
        out_shape=[f32(R, R), f32(R, KD * width), jax.ShapeDtypeStruct((R * width // TILE, TILE), jnp.bfloat16), f32(R, 2 * R)],
        compiler_params=params(),
    )(pieces, fgram, proj, w_rows)
    near = ny * nc
    pieces = exchange(col.reshape(near, col.shape[0] // near, TILE), ("y", "c"))
    pieces = share(jnp.sum(pieces.astype(jnp.float32), axis=0).astype(jnp.bfloat16), "z", nz).astype(jnp.float32)
    pieces = share(jnp.sum(pieces, axis=0), ("y", "c"), near)
    new_v, sums = pl.pallas_call(
        column_kernel,
        in_specs=vmem(3),
        out_specs=vmem(2),
        out_shape=[f32(R, width), f32(nx, R, 2 * R)],
        compiler_params=params(),
    )(pieces.reshape(col.shape), hp, side)
    new_s = pl.pallas_call(
        weight_kernel,
        in_specs=vmem(2),
        out_specs=pl.BlockSpec(memory_space=pltpu.VMEM),
        out_shape=f32(KD, R),
        compiler_params=params(),
    )(exchange(sums, "x"), side)
    return (new_h, new_v, new_s.T)


def solution(mesh):
    traj, nx = mesh.devices.shape
    ny, nc = (4, 2) if traj % 128 == 0 else (2, 2)
    sizes = (ny, traj // (ny * nc), nc, nx)
    fine = Mesh(mesh.devices.reshape(sizes), ("y", "z", "c", "x"))
    traj_axes = ("y", "z", "c")
    return jax.shard_map(
        functools.partial(body, sizes),
        mesh=fine,
        in_specs=(P(traj_axes, "x"), P(traj_axes), P(traj_axes), P(), P(None, "x"), P(None, traj_axes)),
        out_specs=(P(), P(None, "x"), P(None, traj_axes)),
        check_vma=False,
    )
```

```python
import functools

import jax
import jax.numpy as jnp
from jax import lax
from jax.experimental import pallas as pl
from jax.experimental.pallas import tpu as pltpu
from jax.sharding import Mesh, PartitionSpec as P

ITERS = 8
R = 64
TILE = 128
KD = 4
LANES = (((1,), (1,)), ((), ()))

highest = lax.Precision.HIGHEST


def mm(left, right):
    return jnp.dot(left, right, precision=highest, preferred_element_type=jnp.float32)


def mm_t(left, right):
    return lax.dot_general(left, right, LANES, precision=highest, preferred_element_type=jnp.float32)


def halves(value):
    high = value.astype(jnp.bfloat16)
    return high, (value - high.astype(jnp.float32)).astype(jnp.bfloat16)


def mm_halves(left, right, dims=(((1,), (0,)), ((), ()))):
    rows, cols = left.shape[0], right.shape[1 - dims[0][1][0]]
    left = jnp.concatenate(halves(left), axis=0)
    right = jnp.concatenate(halves(right), axis=1 - dims[0][1][0])
    terms = lax.dot_general(left, right, dims, preferred_element_type=jnp.float32)
    return terms[0:rows, 0:cols] + (terms[0:rows, cols:] + terms[rows:, 0:cols])


def eye_mask():
    rows = lax.broadcasted_iota(jnp.int32, (R, R), 0)
    cols = lax.broadcasted_iota(jnp.int32, (R, R), 1)
    return rows == cols


def eliminate(both, block=8):
    rows = lax.broadcasted_iota(jnp.int32, both.shape, 0)
    for k in range(0, R, block):
        col = [jnp.broadcast_to(both[:, k + i : k + i + 1], both.shape) for i in range(block)]
        row = [both[k + i : k + i + 1, :] for i in range(block)]
        piv = [[col[j][k + i : k + i + 1, :] for j in range(block)] for i in range(block)]
        for q in range(0, block, 2):
            inv = 1.0 / (piv[q][q] * piv[q + 1][q + 1] - piv[q][q + 1] * piv[q + 1][q])
            a00, a01 = piv[q + 1][q + 1] * inv, -piv[q][q + 1] * inv
            a10, a11 = -piv[q + 1][q] * inv, piv[q][q] * inv
            new0, new1 = a00 * row[q] + a01 * row[q + 1], a10 * row[q] + a11 * row[q + 1]
            later = range(q + 2, block)
            solved = {
                j: (a00 * piv[q][j] + a01 * piv[q + 1][j], a10 * piv[q][j] + a11 * piv[q + 1][j])
                for j in later
            }
            for i in range(block):
                if i in (q, q + 1):
                    continue
                row[i] = row[i] - (piv[i][q] * new0 + piv[i][q + 1] * new1)
                for j in later:
                    piv[i][j] = piv[i][j] - (piv[i][q] * solved[j][0] + piv[i][q + 1] * solved[j][1])
            row[q], row[q + 1] = new0, new1
            for j in later:
                piv[q][j], piv[q + 1][j] = solved[j]
        rest = both
        for i in range(0, block, 2):
            rest = rest - (col[i] * row[i] + col[i + 1] * row[i + 1])
        for i in range(block):
            rest = jnp.where(rows == k + i, row[i], rest)
        both = rest
    return both


def partial_kernel(v_ref, s_ref, out_ref, v_buf, s_buf, sems):
    count, _, quarter = out_ref.shape
    pieces = 2
    step = count * quarter // pieces
    copies = [pltpu.make_async_copy(v_ref, v_buf, sems.at[pieces])]
    for i in range(pieces):
        rows = pl.ds(i * step, step)
        copies.append(pltpu.make_async_copy(s_ref.at[rows, :], s_buf.at[rows, :], sems.at[i]))
    for copy in copies:
        copy.start()
    copies[0].wait()
    factor_bf = v_buf[...].astype(jnp.bfloat16)
    for i in range(pieces):
        copies[i + 1].wait()
        for peer in range(i * count // pieces, max((i + 1) * count // pieces, i * count // pieces + 1)):
            out_ref[peer] = lax.dot_general(
                factor_bf, s_buf[peer * quarter : (peer + 1) * quarter, :], LANES, preferred_element_type=jnp.float32
            ).astype(jnp.bfloat16)


def three(value):
    high = value.astype(jnp.bfloat16)
    rest = value - high.astype(jnp.float32)
    middle = rest.astype(jnp.bfloat16)
    return high, middle, (rest - middle.astype(jnp.float32)).astype(jnp.bfloat16)


def polar_kernel(
    owner_ref, length_ref, part_ref, h_ref, w_ref, p_ref, send_ref, head_buf, *, peers
):
    rows = p_ref.shape[1]
    slots = rows // TILE
    eye = eye_mask()
    lane = lax.broadcasted_iota(jnp.int32, (1, rows), 1)
    masks = []
    for k in range(KD):
        first = jnp.int32(0)
        for t in range(slots if k > 0 else 0):
            first = first + jnp.where(owner_ref[t] < k, TILE, 0)
        live = (lane >= first) & (lane < first + length_ref[k])
        masks.append(jnp.where(live, 1.0, 0.0).astype(jnp.bfloat16))
    summed = jnp.concatenate([part_ref[peer] for peer in range(peers)], axis=1)
    for k in range(KD):
        p_ref[k * R : (k + 1) * R, :] = summed * masks[k]
    hmat = h_ref[...]
    wmat = w_ref[...].T
    hgram = lax.dot_general(
        hmat, hmat, (((0,), (0,)), ((), ())), precision=highest, preferred_element_type=jnp.float32
    )
    products = lax.dot_general(summed, p_ref[...], LANES, preferred_element_type=jnp.float32)
    wide_eye = jnp.where(
        lax.broadcasted_iota(jnp.int32, (R, 2 * R), 0) == lax.broadcasted_iota(jnp.int32, (R, 2 * R), 1), 1.5, 0.0
    )
    column_rows = [
        jnp.sum(jnp.where(eye, wmat[:, k : k + 1], 0.0), axis=0, keepdims=True) for k in range(KD)
    ]
    both = []
    for k in range(KD):
        column = wmat[:, k : k + 1]
        mix = hmat * column_rows[k]
        product = products[:, k * R : (k + 1) * R]
        gram = mm_t(mm(mix, product), mix)
        energy = jnp.sum(product * (hgram * column * column_rows[k]), keepdims=True)
        scale = lax.rsqrt(energy + 1e-06)
        both.append(jnp.concatenate([gram * (scale * scale), mix * scale], axis=1))
    for iteration in range(ITERS):
        steps = [wide_eye - 0.5 * pair for pair in both]
        both = [mm_halves(step[:, 0:R], pair) for step, pair in zip(steps, both)]
        if iteration < ITERS - 1:
            next_grams = [mm_halves(pair[:, 0:R], step) for step, pair in zip(steps, both)]
            first_half = lax.broadcasted_iota(jnp.int32, (R, 2 * R), 1) < R
            both = [jnp.where(first_half, gram, pair) for gram, pair in zip(next_grams, both)]
    parts = [three(pair[:, R : 2 * R]) for pair in both]
    turn_rows = jnp.concatenate(
        [jnp.concatenate([parts[k][i] for k in range(KD)], axis=1) for i in range(3)], axis=0
    )
    chunk = 2 * TILE
    for first in range(0, rows, chunk):
        cols = slice(first, first + chunk)
        terms = jnp.dot(turn_rows, p_ref[:, cols], preferred_element_type=jnp.float32)
        polar = (terms[0:R] + (terms[R : 2 * R] + terms[2 * R : 3 * R])).astype(jnp.bfloat16)
        for k in range(KD):
            p_ref[k * R : (k + 1) * R, cols] = polar * masks[k][:, cols]
    heads = lax.dot_general(p_ref[...], summed, LANES, preferred_element_type=jnp.float32)
    head = jnp.zeros((R, R), jnp.float32)
    for k in range(KD):
        head = head + heads[k * R : (k + 1) * R, :] * column_rows[k]
    head_buf[...] = head
    share_rows = R // peers
    first = pl.multiple_of(lax.axis_index("x") * share_rows, share_rows)
    high, middle, low = [term.astype(jnp.float32) for term in three(w_ref[...])]
    send_ref[...] = jnp.concatenate(
        [
            fold(head_buf[pl.ds(first, share_rows), :]),
            jnp.concatenate([high, middle], axis=1),
            jnp.concatenate([low, jnp.zeros_like(low)], axis=1),
        ],
        axis=0,
    ).astype(jnp.bfloat16)


def fold(value):
    half = value.shape[0] // 2
    return jnp.concatenate([value[0:half], value[half:]], axis=1)


def unfold(value):
    return jnp.concatenate([value[:, 0:R], value[:, R : 2 * R]], axis=0)


def wide_halves(value):
    return jnp.concatenate([half.astype(jnp.float32) for half in halves(value)], axis=1)


def middle_kernel(in_ref, v_ref, out_ref, w_buf, gram_buf, *, sizes):
    ny, nz, nc, nx = sizes
    h_rows = R // nx // 2
    head = jnp.zeros((h_rows, 2 * R), jnp.float32)
    for peer in range(nz):
        value = in_ref[peer].astype(jnp.float32)
        head = head + value[0:h_rows]
        first, last = value[h_rows : h_rows + KD], value[h_rows + KD :]
        w_buf[peer * KD : (peer + 1) * KD, :] = first[:, 0:R] + (first[:, R:] + last[:, 0:R])
    weights = w_buf[...]
    gram_buf[0:R, :] = lax.dot_general(
        weights, weights, (((0,), (0,)), ((), ())), precision=highest, preferred_element_type=jnp.float32
    )
    vmat = v_ref[...]
    gram_buf[R : 2 * R, :] = mm_t(vmat, vmat)
    w_rows, v_rows = R // nx, R // (ny * nc)
    place = lax.axis_index("y") * nc + lax.axis_index("c")
    w_first = pl.multiple_of(lax.axis_index("x") * w_rows, w_rows)
    v_first = pl.multiple_of(R + place * v_rows, v_rows)
    parts = [
        head,
        wide_halves(gram_buf[pl.ds(w_first, w_rows), :]),
        wide_halves(gram_buf[pl.ds(v_first, v_rows), :]),
    ]
    value = jnp.concatenate(parts, axis=0).astype(jnp.bfloat16)
    for peer in range(out_ref.shape[0]):
        out_ref[peer] = value


def head_kernel(pack_ref, p_ref, s_ref, w_ref, newh_ref, hp_ref, col_ref, side_ref, *, sizes):
    ny, _, nc, nx = sizes
    h_rows, w_rows, v_rows = R // nx // 2, R // nx, R // (ny * nc)
    w_last = h_rows + w_rows
    h_parts, w_parts, v_parts = [0.0] * nx, [0.0] * nx, [0.0] * (ny * nc)
    for peer in range(pack_ref.shape[0]):
        value = pack_ref[peer].astype(jnp.float32)
        place, x = divmod(peer, nx)
        h_parts[x] = h_parts[x] + value[0:h_rows]
        w_parts[x] = w_parts[x] + value[h_rows:w_last]
        v_parts[place] = v_parts[place] + value[w_last : w_last + v_rows]
    head = jnp.concatenate([unfold(part) for part in h_parts], axis=0)
    wgram, fgram = [
        jnp.concatenate([part[:, 0:R] + part[:, R:] for part in parts], axis=0) for parts in (w_parts, v_parts)
    ]
    newh_t = eliminate(jnp.concatenate([fgram * wgram, head.T], axis=1))[:, R:]
    newh_ref[...] = newh_t.T
    wmat = w_ref[...].T
    projected = jnp.dot(p_ref[...], s_ref[...], preferred_element_type=jnp.float32)
    width = projected.shape[1]
    projected = jnp.concatenate([projected[k * R : (k + 1) * R, :] for k in range(KD)], axis=1)
    hp = mm_halves(newh_t, projected)
    hp_ref[...] = hp
    col = hp[:, 0:width] * wmat[:, 0:1]
    for k in range(1, KD):
        col = col + hp[:, k * width : (k + 1) * width] * wmat[:, k : k + 1]
    for half in range(width // TILE):
        col_ref[half * R : (half + 1) * R, :] = col[:, half * TILE : (half + 1) * TILE].astype(jnp.bfloat16)
    hgram = mm_t(newh_t, newh_t)
    inverse = eliminate(jnp.concatenate([hgram * wgram, jnp.where(eye_mask(), 1.0, 0.0)], axis=1))[:, R:]
    side_ref[...] = jnp.concatenate([hgram, inverse], axis=1)


def column_kernel(col_ref, hp_ref, inverse_ref, newv_ref, out_ref):
    halves = col_ref.shape[0] // R
    col = jnp.concatenate([col_ref[half * R : (half + 1) * R, :] for half in range(halves)], axis=1)
    newv = mm(inverse_ref[:, R : 2 * R], col)
    newv_ref[...] = newv
    width = newv.shape[1]
    eye = eye_mask()
    row = lax.broadcasted_iota(jnp.int32, (8, R), 0)
    terms = jnp.zeros((8, R), jnp.float32)
    for k in range(KD):
        sums = jnp.sum(hp_ref[:, k * width : (k + 1) * width] * newv, axis=1, keepdims=True)
        terms = jnp.where(row == k, jnp.sum(jnp.where(eye, sums, 0.0), axis=0, keepdims=True), terms)
    value = jnp.concatenate(
        [fold(mm_t(newv, newv)), jnp.concatenate([terms, jnp.zeros_like(terms)], axis=1)], axis=0
    )
    for peer in range(out_ref.shape[0]):
        out_ref[peer] = value


def weight_kernel(in_ref, side_ref, out_ref):
    value = in_ref[0]
    for peer in range(1, in_ref.shape[0]):
        value = value + in_ref[peer]
    gram = side_ref[:, 0:R] * unfold(value[0 : R // 2])
    terms = value[R // 2 :, 0:R].T
    solved = eliminate(jnp.concatenate([gram, terms, jnp.zeros((R, R - 8), jnp.float32)], axis=1))
    out_ref[...] = solved[:, R : R + KD].T


def vmem(count):
    return [pl.BlockSpec(memory_space=pltpu.VMEM)] * count


def params(mib=48):
    return pltpu.CompilerParams(vmem_limit_bytes=mib * 1024 * 1024)


def f32(*shape):
    return jax.ShapeDtypeStruct(shape, jnp.float32)


def exchange(value, axes):
    return lax.all_to_all(value, axes, 0, 0, tiled=True)


def share(value, axes, peers):
    return exchange(jnp.broadcast_to(value[None], (peers,) + value.shape), axes)


def body(sizes, series, lengths, tile_owner, factor_h, factor_v, weights_s):
    ny, nz, nc, nx = sizes
    rows, width = series.shape
    slots = tile_owner.shape[0]
    quarter = rows // nx
    w_rows = weights_s.T
    parts = pl.pallas_call(
        partial_kernel,
        in_specs=[pl.BlockSpec(memory_space=pltpu.HBM)] * 2,
        out_specs=pl.BlockSpec(memory_space=pltpu.VMEM),
        out_shape=jax.ShapeDtypeStruct((nx, R, quarter), jnp.bfloat16),
        scratch_shapes=[
            pltpu.VMEM((R, width), jnp.float32),
            pltpu.VMEM((rows, width), jnp.bfloat16),
            pltpu.SemaphoreType.DMA((nx + 1,)),
        ],
        compiler_params=params(63),
    )(factor_v, series)
    parts = jnp.sum(exchange(parts, "x").astype(jnp.float32), axis=0).astype(jnp.bfloat16)
    parts = share(parts, "x", nx)
    polar, send = pl.pallas_call(
        functools.partial(polar_kernel, peers=nx),
        in_specs=[pl.BlockSpec(memory_space=pltpu.SMEM)] * 2 + vmem(3),
        out_specs=vmem(2),
        out_shape=[
            jax.ShapeDtypeStruct((KD * R, rows), jnp.bfloat16),
            jax.ShapeDtypeStruct((R // nx // 2 + 2 * KD, 2 * R), jnp.bfloat16),
        ],
        scratch_shapes=[
            pltpu.VMEM((R, R), jnp.float32),
        ],
        compiler_params=params(),
    )(tile_owner, lengths, parts, factor_h, w_rows)
    near = ny * nc * nx
    share_rows = R // nx // 2 + R // nx + R // (ny * nc)
    pieces = pl.pallas_call(
        functools.partial(middle_kernel, sizes=sizes),
        in_specs=vmem(2),
        out_specs=pl.BlockSpec(memory_space=pltpu.VMEM),
        out_shape=jax.ShapeDtypeStruct((near, share_rows, 2 * R), jnp.bfloat16),
        scratch_shapes=[pltpu.VMEM((nz * KD, R), jnp.float32), pltpu.VMEM((2 * R, R), jnp.float32)],
        compiler_params=params(),
    )(share(send, "z", nz), factor_v)
    pieces = exchange(pieces, ("y", "c", "x"))
    new_h, hp, col, side = pl.pallas_call(
        functools.partial(head_kernel, sizes=sizes),
        in_specs=vmem(4),
        out_specs=vmem(4),
        out_shape=[f32(R, R), f32(R, KD * width), jax.ShapeDtypeStruct((R * width // TILE, TILE), jnp.bfloat16), f32(R, 2 * R)],
        compiler_params=params(),
    )(pieces, polar, series, w_rows)
    near = ny * nc
    pieces = exchange(col.reshape(near, col.shape[0] // near, TILE), ("y", "c"))
    pieces = share(jnp.sum(pieces.astype(jnp.float32), axis=0).astype(jnp.bfloat16), "z", nz).astype(jnp.float32)
    pieces = share(jnp.sum(pieces, axis=0), ("y", "c"), near)
    new_v, sums = pl.pallas_call(
        column_kernel,
        in_specs=vmem(3),
        out_specs=vmem(2),
        out_shape=[f32(R, width), f32(nx, R // 2 + 8, 2 * R)],
        compiler_params=params(),
    )(pieces.reshape(col.shape), hp, side)
    new_s = pl.pallas_call(
        weight_kernel,
        in_specs=vmem(2),
        out_specs=pl.BlockSpec(memory_space=pltpu.VMEM),
        out_shape=f32(KD, R),
        compiler_params=params(),
    )(exchange(sums, "x"), side)
    return (new_h, new_v, new_s.T)


def solution(mesh):
    traj, nx = mesh.devices.shape
    ny, nc = (4, 2) if traj % 128 == 0 else (2, 2)
    sizes = (ny, traj // (ny * nc), nc, nx)
    fine = Mesh(mesh.devices.reshape(sizes), ("y", "z", "c", "x"))
    traj_axes = ("y", "z", "c")
    return jax.shard_map(
        functools.partial(body, sizes),
        mesh=fine,
        in_specs=(P(traj_axes, "x"), P(traj_axes), P(traj_axes), P(), P(None, "x"), P(None, traj_axes)),
        out_specs=(P(), P(None, "x"), P(None, traj_axes)),
        check_vma=False,
    )
```

```python
import functools

import jax
import jax.numpy as jnp
from jax import lax
from jax.experimental import pallas as pl
from jax.experimental.pallas import tpu as pltpu
from jax.sharding import Mesh, PartitionSpec as P

ITERS = 8
R = 64
TILE = 128
KD = 4
LANES = (((1,), (1,)), ((), ()))

highest = lax.Precision.HIGHEST


def mm(left, right):
    return jnp.dot(left, right, precision=highest, preferred_element_type=jnp.float32)


def mm_t(left, right):
    return lax.dot_general(left, right, LANES, precision=highest, preferred_element_type=jnp.float32)


def halves(value):
    high = value.astype(jnp.bfloat16)
    return high, (value - high.astype(jnp.float32)).astype(jnp.bfloat16)


def mm_halves(left, right, dims=(((1,), (0,)), ((), ()))):
    rows, cols = left.shape[0], right.shape[1 - dims[0][1][0]]
    left = jnp.concatenate(halves(left), axis=0)
    right = jnp.concatenate(halves(right), axis=1 - dims[0][1][0])
    terms = lax.dot_general(left, right, dims, preferred_element_type=jnp.float32)
    return terms[0:rows, 0:cols] + (terms[0:rows, cols:] + terms[rows:, 0:cols])


def eye_mask():
    rows = lax.broadcasted_iota(jnp.int32, (R, R), 0)
    cols = lax.broadcasted_iota(jnp.int32, (R, R), 1)
    return rows == cols


def eliminate(both, block=8):
    rows = lax.broadcasted_iota(jnp.int32, both.shape, 0)
    for k in range(0, R, block):
        col = [jnp.broadcast_to(both[:, k + i : k + i + 1], both.shape) for i in range(block)]
        row = [both[k + i : k + i + 1, :] for i in range(block)]
        piv = [[col[j][k + i : k + i + 1, :] for j in range(block)] for i in range(block)]
        for q in range(0, block, 2):
            inv = 1.0 / (piv[q][q] * piv[q + 1][q + 1] - piv[q][q + 1] * piv[q + 1][q])
            a00, a01 = piv[q + 1][q + 1] * inv, -piv[q][q + 1] * inv
            a10, a11 = -piv[q + 1][q] * inv, piv[q][q] * inv
            new0, new1 = a00 * row[q] + a01 * row[q + 1], a10 * row[q] + a11 * row[q + 1]
            later = range(q + 2, block)
            solved = {
                j: (a00 * piv[q][j] + a01 * piv[q + 1][j], a10 * piv[q][j] + a11 * piv[q + 1][j])
                for j in later
            }
            for i in range(block):
                if i in (q, q + 1):
                    continue
                row[i] = row[i] - (piv[i][q] * new0 + piv[i][q + 1] * new1)
                for j in later:
                    piv[i][j] = piv[i][j] - (piv[i][q] * solved[j][0] + piv[i][q + 1] * solved[j][1])
            row[q], row[q + 1] = new0, new1
            for j in later:
                piv[q][j], piv[q + 1][j] = solved[j]
        rest = both
        for i in range(0, block, 2):
            rest = rest - (col[i] * row[i] + col[i + 1] * row[i + 1])
        for i in range(block):
            rest = jnp.where(rows == k + i, row[i], rest)
        both = rest
    return both


def partial_kernel(v_ref, s_ref, out_ref, v_buf, s_buf, sems):
    count, _, quarter = out_ref.shape
    pieces = 2
    step = count * quarter // pieces
    copies = [pltpu.make_async_copy(v_ref, v_buf, sems.at[pieces])]
    for i in range(pieces):
        rows = pl.ds(i * step, step)
        copies.append(pltpu.make_async_copy(s_ref.at[rows, :], s_buf.at[rows, :], sems.at[i]))
    for copy in copies:
        copy.start()
    copies[0].wait()
    factor_bf = v_buf[...].astype(jnp.bfloat16)
    for i in range(pieces):
        copies[i + 1].wait()
        for peer in range(i * count // pieces, max((i + 1) * count // pieces, i * count // pieces + 1)):
            out_ref[peer] = lax.dot_general(
                factor_bf, s_buf[peer * quarter : (peer + 1) * quarter, :], LANES, preferred_element_type=jnp.float32
            ).astype(jnp.bfloat16)


def three(value):
    high = value.astype(jnp.bfloat16)
    rest = value - high.astype(jnp.float32)
    middle = rest.astype(jnp.bfloat16)
    return high, middle, (rest - middle.astype(jnp.float32)).astype(jnp.bfloat16)


def polar_kernel(
    owner_ref, length_ref, part_ref, s_ref, h_ref, w_ref, proj_ref, send_ref, p_ref, head_buf, *, peers
):
    rows, width = s_ref.shape
    slots = rows // TILE
    eye = eye_mask()
    lane = lax.broadcasted_iota(jnp.int32, (1, rows), 1)
    masks = []
    for k in range(KD):
        first = jnp.int32(0)
        for t in range(slots if k > 0 else 0):
            first = first + jnp.where(owner_ref[t] < k, TILE, 0)
        live = (lane >= first) & (lane < first + length_ref[k])
        masks.append(jnp.where(live, 1.0, 0.0).astype(jnp.bfloat16))
    summed = jnp.concatenate([part_ref[peer] for peer in range(peers)], axis=1)
    for k in range(KD):
        p_ref[k * R : (k + 1) * R, :] = summed * masks[k]
    hmat = h_ref[...]
    wmat = w_ref[...].T
    hgram = lax.dot_general(
        hmat, hmat, (((0,), (0,)), ((), ())), precision=highest, preferred_element_type=jnp.float32
    )
    products = lax.dot_general(summed, p_ref[...], LANES, preferred_element_type=jnp.float32)
    wide_eye = jnp.where(
        lax.broadcasted_iota(jnp.int32, (R, 2 * R), 0) == lax.broadcasted_iota(jnp.int32, (R, 2 * R), 1), 1.5, 0.0
    )
    column_rows = [
        jnp.sum(jnp.where(eye, wmat[:, k : k + 1], 0.0), axis=0, keepdims=True) for k in range(KD)
    ]
    both = []
    for k in range(KD):
        column = wmat[:, k : k + 1]
        mix = hmat * column_rows[k]
        product = products[:, k * R : (k + 1) * R]
        gram = mm_t(mm(mix, product), mix)
        energy = jnp.sum(product * (hgram * column * column_rows[k]), keepdims=True)
        scale = lax.rsqrt(energy + 1e-06)
        both.append(jnp.concatenate([gram * (scale * scale), mix * scale], axis=1))
    for iteration in range(ITERS):
        steps = [wide_eye - 0.5 * pair for pair in both]
        both = [mm_halves(step[:, 0:R], pair) for step, pair in zip(steps, both)]
        if iteration < ITERS - 1:
            next_grams = [mm_halves(pair[:, 0:R], step) for step, pair in zip(steps, both)]
            first_half = lax.broadcasted_iota(jnp.int32, (R, 2 * R), 1) < R
            both = [jnp.where(first_half, gram, pair) for gram, pair in zip(next_grams, both)]
    parts = [three(pair[:, R : 2 * R]) for pair in both]
    turn_rows = jnp.concatenate(
        [jnp.concatenate([parts[k][i] for k in range(KD)], axis=1) for i in range(3)], axis=0
    )
    chunk = 2 * TILE
    for first in range(0, rows, chunk):
        cols = slice(first, first + chunk)
        terms = jnp.dot(turn_rows, p_ref[:, cols], preferred_element_type=jnp.float32)
        polar = (terms[0:R] + (terms[R : 2 * R] + terms[2 * R : 3 * R])).astype(jnp.bfloat16)
        for k in range(KD):
            p_ref[k * R : (k + 1) * R, cols] = polar * masks[k][:, cols]
    projected = jnp.dot(p_ref[...], s_ref[...], preferred_element_type=jnp.float32)
    heads = lax.dot_general(p_ref[...], summed, LANES, preferred_element_type=jnp.float32)
    head = jnp.zeros((R, R), jnp.float32)
    for k in range(KD):
        proj_ref[:, k * width : (k + 1) * width] = projected[k * R : (k + 1) * R, :]
        head = head + heads[k * R : (k + 1) * R, :] * column_rows[k]
    head_buf[...] = head
    share_rows = R // peers
    first = pl.multiple_of(lax.axis_index("x") * share_rows, share_rows)
    high, middle, low = [term.astype(jnp.float32) for term in three(w_ref[...])]
    send_ref[...] = jnp.concatenate(
        [
            fold(head_buf[pl.ds(first, share_rows), :]),
            jnp.concatenate([high, middle], axis=1),
            jnp.concatenate([low, jnp.zeros_like(low)], axis=1),
        ],
        axis=0,
    ).astype(jnp.bfloat16)


def fold(value):
    half = value.shape[0] // 2
    return jnp.concatenate([value[0:half], value[half:]], axis=1)


def unfold(value):
    return jnp.concatenate([value[:, 0:R], value[:, R : 2 * R]], axis=0)


def wide_halves(value):
    return jnp.concatenate([half.astype(jnp.float32) for half in halves(value)], axis=1)


def middle_kernel(in_ref, v_ref, out_ref, w_buf, gram_buf, *, sizes):
    ny, nz, nc, nx = sizes
    h_rows = R // nx // 2
    head = jnp.zeros((h_rows, 2 * R), jnp.float32)
    for peer in range(nz):
        value = in_ref[peer].astype(jnp.float32)
        head = head + value[0:h_rows]
        first, last = value[h_rows : h_rows + KD], value[h_rows + KD :]
        w_buf[peer * KD : (peer + 1) * KD, :] = first[:, 0:R] + (first[:, R:] + last[:, 0:R])
    weights = w_buf[...]
    gram_buf[0:R, :] = lax.dot_general(
        weights, weights, (((0,), (0,)), ((), ())), precision=highest, preferred_element_type=jnp.float32
    )
    vmat = v_ref[...]
    gram_buf[R : 2 * R, :] = mm_t(vmat, vmat)
    w_rows, v_rows = R // nx, R // (ny * nc)
    place = lax.axis_index("y") * nc + lax.axis_index("c")
    w_first = pl.multiple_of(lax.axis_index("x") * w_rows, w_rows)
    v_first = pl.multiple_of(R + place * v_rows, v_rows)
    parts = [
        head,
        wide_halves(gram_buf[pl.ds(w_first, w_rows), :]),
        wide_halves(gram_buf[pl.ds(v_first, v_rows), :]),
    ]
    value = jnp.concatenate(parts, axis=0).astype(jnp.bfloat16)
    for peer in range(out_ref.shape[0]):
        out_ref[peer] = value


def head_kernel(pack_ref, proj_ref, w_ref, newh_ref, hp_ref, col_ref, side_ref, *, sizes):
    ny, _, nc, nx = sizes
    h_rows, w_rows, v_rows = R // nx // 2, R // nx, R // (ny * nc)
    w_last = h_rows + w_rows
    h_parts, w_parts, v_parts = [0.0] * nx, [0.0] * nx, [0.0] * (ny * nc)
    for peer in range(pack_ref.shape[0]):
        value = pack_ref[peer].astype(jnp.float32)
        place, x = divmod(peer, nx)
        h_parts[x] = h_parts[x] + value[0:h_rows]
        w_parts[x] = w_parts[x] + value[h_rows:w_last]
        v_parts[place] = v_parts[place] + value[w_last : w_last + v_rows]
    head = jnp.concatenate([unfold(part) for part in h_parts], axis=0)
    wgram, fgram = [
        jnp.concatenate([part[:, 0:R] + part[:, R:] for part in parts], axis=0) for parts in (w_parts, v_parts)
    ]
    newh_t = eliminate(jnp.concatenate([fgram * wgram, head.T], axis=1))[:, R:]
    newh_ref[...] = newh_t.T
    wmat = w_ref[...].T
    hp = mm_halves(newh_t, proj_ref[...])
    hp_ref[...] = hp
    width = hp.shape[1] // KD
    col = hp[:, 0:width] * wmat[:, 0:1]
    for k in range(1, KD):
        col = col + hp[:, k * width : (k + 1) * width] * wmat[:, k : k + 1]
    for half in range(width // TILE):
        col_ref[half * R : (half + 1) * R, :] = col[:, half * TILE : (half + 1) * TILE].astype(jnp.bfloat16)
    hgram = mm_t(newh_t, newh_t)
    inverse = eliminate(jnp.concatenate([hgram * wgram, jnp.where(eye_mask(), 1.0, 0.0)], axis=1))[:, R:]
    side_ref[...] = jnp.concatenate([hgram, inverse], axis=1)


def column_kernel(col_ref, hp_ref, inverse_ref, newv_ref, out_ref):
    halves = col_ref.shape[0] // R
    col = jnp.concatenate([col_ref[half * R : (half + 1) * R, :] for half in range(halves)], axis=1)
    newv = mm(inverse_ref[:, R : 2 * R], col)
    newv_ref[...] = newv
    width = newv.shape[1]
    eye = eye_mask()
    row = lax.broadcasted_iota(jnp.int32, (8, R), 0)
    terms = jnp.zeros((8, R), jnp.float32)
    for k in range(KD):
        sums = jnp.sum(hp_ref[:, k * width : (k + 1) * width] * newv, axis=1, keepdims=True)
        terms = jnp.where(row == k, jnp.sum(jnp.where(eye, sums, 0.0), axis=0, keepdims=True), terms)
    value = jnp.concatenate(
        [fold(mm_t(newv, newv)), jnp.concatenate([terms, jnp.zeros_like(terms)], axis=1)], axis=0
    )
    for peer in range(out_ref.shape[0]):
        out_ref[peer] = value


def weight_kernel(in_ref, side_ref, out_ref):
    value = in_ref[0]
    for peer in range(1, in_ref.shape[0]):
        value = value + in_ref[peer]
    gram = side_ref[:, 0:R] * unfold(value[0 : R // 2])
    terms = value[R // 2 :, 0:R].T
    solved = eliminate(jnp.concatenate([gram, terms, jnp.zeros((R, R - 8), jnp.float32)], axis=1))
    out_ref[...] = solved[:, R : R + KD].T


def vmem(count):
    return [pl.BlockSpec(memory_space=pltpu.VMEM)] * count


def params(mib=48):
    return pltpu.CompilerParams(vmem_limit_bytes=mib * 1024 * 1024)


def f32(*shape):
    return jax.ShapeDtypeStruct(shape, jnp.float32)


def exchange(value, axes):
    return lax.all_to_all(value, axes, 0, 0, tiled=True)


def share(value, axes, peers):
    return exchange(jnp.broadcast_to(value[None], (peers,) + value.shape), axes)


def body(sizes, series, lengths, tile_owner, factor_h, factor_v, weights_s):
    ny, nz, nc, nx = sizes
    rows, width = series.shape
    slots = tile_owner.shape[0]
    quarter = rows // nx
    w_rows = weights_s.T
    parts = pl.pallas_call(
        partial_kernel,
        in_specs=[pl.BlockSpec(memory_space=pltpu.HBM)] * 2,
        out_specs=pl.BlockSpec(memory_space=pltpu.VMEM),
        out_shape=jax.ShapeDtypeStruct((nx, R, quarter), jnp.bfloat16),
        scratch_shapes=[
            pltpu.VMEM((R, width), jnp.float32),
            pltpu.VMEM((rows, width), jnp.bfloat16),
            pltpu.SemaphoreType.DMA((nx + 1,)),
        ],
        compiler_params=params(63),
    )(factor_v, series)
    parts = jnp.sum(exchange(parts, "x").astype(jnp.float32), axis=0).astype(jnp.bfloat16)
    parts = share(parts, "x", nx)
    proj, send = pl.pallas_call(
        functools.partial(polar_kernel, peers=nx),
        in_specs=[pl.BlockSpec(memory_space=pltpu.SMEM)] * 2 + vmem(4),
        out_specs=vmem(2),
        out_shape=[f32(R, KD * width), jax.ShapeDtypeStruct((R // nx // 2 + 2 * KD, 2 * R), jnp.bfloat16)],
        scratch_shapes=[
            pltpu.VMEM((KD * R, rows), jnp.bfloat16),
            pltpu.VMEM((R, R), jnp.float32),
        ],
        compiler_params=params(),
    )(tile_owner, lengths, parts, series, factor_h, w_rows)
    near = ny * nc * nx
    share_rows = R // nx // 2 + R // nx + R // (ny * nc)
    pieces = pl.pallas_call(
        functools.partial(middle_kernel, sizes=sizes),
        in_specs=vmem(2),
        out_specs=pl.BlockSpec(memory_space=pltpu.VMEM),
        out_shape=jax.ShapeDtypeStruct((near, share_rows, 2 * R), jnp.bfloat16),
        scratch_shapes=[pltpu.VMEM((nz * KD, R), jnp.float32), pltpu.VMEM((2 * R, R), jnp.float32)],
        compiler_params=params(),
    )(share(send, "z", nz), factor_v)
    pieces = exchange(pieces, ("y", "c", "x"))
    new_h, hp, col, side = pl.pallas_call(
        functools.partial(head_kernel, sizes=sizes),
        in_specs=vmem(3),
        out_specs=vmem(4),
        out_shape=[f32(R, R), f32(R, KD * width), jax.ShapeDtypeStruct((R * width // TILE, TILE), jnp.bfloat16), f32(R, 2 * R)],
        compiler_params=params(),
    )(pieces, proj, w_rows)
    near = ny * nc
    pieces = exchange(col.reshape(near, col.shape[0] // near, TILE), ("y", "c"))
    pieces = share(jnp.sum(pieces.astype(jnp.float32), axis=0).astype(jnp.bfloat16), "z", nz).astype(jnp.float32)
    pieces = share(jnp.sum(pieces, axis=0), ("y", "c"), near)
    new_v, sums = pl.pallas_call(
        column_kernel,
        in_specs=vmem(3),
        out_specs=vmem(2),
        out_shape=[f32(R, width), f32(nx, R // 2 + 8, 2 * R)],
        compiler_params=params(),
    )(pieces.reshape(col.shape), hp, side)
    new_s = pl.pallas_call(
        weight_kernel,
        in_specs=vmem(2),
        out_specs=pl.BlockSpec(memory_space=pltpu.VMEM),
        out_shape=f32(KD, R),
        compiler_params=params(),
    )(exchange(sums, "x"), side)
    return (new_h, new_v, new_s.T)


def solution(mesh):
    traj, nx = mesh.devices.shape
    ny, nc = (4, 2) if traj % 128 == 0 else (2, 2)
    sizes = (ny, traj // (ny * nc), nc, nx)
    fine = Mesh(mesh.devices.reshape(sizes), ("y", "z", "c", "x"))
    traj_axes = ("y", "z", "c")
    return jax.shard_map(
        functools.partial(body, sizes),
        mesh=fine,
        in_specs=(P(traj_axes, "x"), P(traj_axes), P(traj_axes), P(), P(None, "x"), P(None, traj_axes)),
        out_specs=(P(), P(None, "x"), P(None, traj_axes)),
        check_vma=False,
    )
```
